256 devices in a mesh: ctx: 32 (over y, x, z_hi), fsdp: 8 (over z_lo, core).
Axes of the slice: x: 4, y: 4, z: 8 (z_hi: 2, z_lo: 4; z = z_hi * 4 + z_lo), core: 2. Of those that a mesh axis runs over, the one named last changes fastest.
Arguments:
- proj: bfloat16 [8, 4096, 12288], P('fsdp', 'ctx'), may hold values from -6 to 6
- short_taps: float32 [7, 12288], P(None, 'fsdp'), may hold values from -2 to 2
- long_filter: float32 [128, 256], P(None, 'fsdp'), may hold values from -0.5 to 0.5
- skip: float32 [4096], P('fsdp'), may hold values from -3 to 3
- grad_out: bfloat16 [8, 4096, 4096], P('fsdp', 'ctx'), may hold values from -6 to 6
- starts: int32 [8, 32, 4], P('fsdp', 'ctx'), may hold values from 0 to 128, as said below
Outputs:
- mixed_out: bfloat16 [8, 4096, 4096], P('fsdp', 'ctx')
- grad_proj: bfloat16 [8, 4096, 12288], P('fsdp', 'ctx')
- grad_short: float32 [7, 12288], P(None, 'fsdp')
- grad_long: float32 [128, 256], P(None, 'fsdp')
- grad_skip: float32 [4096], P('fsdp')
The draws below stay inside these ranges and needn't reach their ends.
Inputs may be any that keep to these rules, and one draw needn't show every extreme that they name: Each list holds positions, within one device's 128 positions, at which documents start, increasing and without repeats; entries equal to 128 are empty and come after all others. Every window's first position starts a document.
All inputs are finite; a program needn't handle non-finite values.
Results may differ from the reference program's by a relative error of at most 0.007.
Values may be sent and summed in bfloat16 or wider, within the bound.
No kernel may reach another device: no remote copies, remote signals or barrier semaphores. Data moves between devices by JAX's collectives and lax.ppermute only.
A program may use at most 128 MiB of HBM per device.

```python
import jax
import jax.numpy as jnp
from jax import lax

C = 4096
GROUP = 16
LEN = 128
SHORT = 7
NB = 4
TOK_DEV = 128
GROUPS = 256
SHARDS = 32
WINDOWS = 8
SEQ = 4096


def draw_starts(key, part):
    key = jax.random.fold_in(key, 7)
    order_key, count_key, emptied_key = jax.random.split(key, 3)
    scores = jax.random.randint(order_key, (WINDOWS, SHARDS, TOK_DEV), 0, 1 << 20) * TOK_DEV
    scores = scores + jnp.arange(TOK_DEV, dtype=jnp.int32)
    picked = jnp.sort(jnp.argsort(scores, axis=-1)[..., :NB].astype(jnp.int32), axis=-1)
    picked = picked.at[:, 0, 0].set(0)
    counts = jax.random.randint(count_key, (WINDOWS, SHARDS), 0, NB + 1)
    counts = counts.at[:, 0].set(jnp.maximum(counts[:, 0], 1))
    emptied = jax.random.randint(emptied_key, (WINDOWS, 1), 1, SHARDS)
    counts = jnp.where(jnp.arange(SHARDS, dtype=jnp.int32)[None, :] == emptied, 0, counts)
    slots = jnp.arange(NB, dtype=jnp.int32)
    return jnp.where(slots[None, None, :] < counts[..., None], picked, TOK_DEV).astype(jnp.int32)


def block_levels(key, extent, cuts, smallest, largest):
    gain, own = 1.0, jax.random.fold_in(key, 6)
    for position, parts in cuts:
        heights = jnp.exp(jax.random.uniform(jax.random.fold_in(own, position), (parts,), jnp.float32, smallest / len(cuts), largest / len(cuts)))
        gain = gain * jnp.repeat(heights, extent[position] // parts).reshape([-1 if axis == position else 1 for axis in range(len(extent))])
    return gain


def noise(own_key, extent, spread, bound, shards=(), kind=jnp.bfloat16):
    values = jax.random.normal(own_key, extent, jnp.float32) * spread
    if len(shards) > 0:
        values = block_levels(own_key, extent, shards, -0.22, 0.18) * values
    return jnp.clip(values, min=-bound, max=bound).astype(kind)


def setup_inputs(seed: int = 0) -> dict:
    arg_keys = jax.random.split(jax.random.key(seed), 7)
    proj = noise(arg_keys[0], (WINDOWS, SEQ, 3 * C), 1.0, 6.0, ((0, 8), (1, 32)))
    short_taps = noise(arg_keys[1], (SHORT, 3 * C), SHORT ** -0.5, 2.0, ((1, 8),), jnp.float32)
    long_filter = noise(arg_keys[2], (LEN, GROUPS), LEN ** -0.5, 0.5, ((1, 8),), jnp.float32)
    skip = noise(arg_keys[3], (C,), 1.0, 3.0, ((0, 8),), jnp.float32)
    grad_out = noise(arg_keys[4], (WINDOWS, SEQ, C), 1.0, 6.0, ((0, 8), (1, 32)))
    starts = draw_starts(jax.random.fold_in(arg_keys[6], 71), 0)
    return dict(proj=proj, short_taps=short_taps, long_filter=long_filter, skip=skip, grad_out=grad_out, starts=starts)


def rounded(values):
    return lax.optimization_barrier(values.astype(jnp.bfloat16)).astype(jnp.float32)


def last_starts(starts_w):
    offsets = (jnp.arange(SHARDS, dtype=jnp.int32) * TOK_DEV)[:, None]
    marked = jnp.where(starts_w < TOK_DEV, starts_w + offsets, -1).reshape(-1)
    places = jnp.arange(SEQ, dtype=jnp.int32)
    is_start = jnp.any(marked[:, None] == places[None, :], axis=0)
    return lax.cummax(jnp.where(is_start, places, -1), axis=0)


def band_rows(filt_rows, rows_count, cols_count, lag_base):
    lag_table = jnp.arange(rows_count, dtype=jnp.int32)[:, None] - jnp.arange(cols_count, dtype=jnp.int32)[None, :] + lag_base
    inside = (lag_table >= 0) & (lag_table < LEN)
    picked = filt_rows[:, jnp.clip(lag_table, 0, LEN - 1)]
    return jnp.where(inside[None], picked, 0.0)


def lag_totals(product, rows_count, cols_count):
    groups = product.shape[0]
    flattened = product.reshape(groups, rows_count * cols_count)
    flattened = jnp.concatenate([flattened, jnp.zeros((groups, rows_count), product.dtype)], axis=1)
    totals = jnp.sum(flattened.reshape(groups, rows_count, cols_count + 1), axis=1)
    return totals[:, LEN:0:-1]


def reference(proj, short_taps, long_filter, skip, grad_out, starts):
    filt_rows = rounded(long_filter).T
    win_rows = TOK_DEV + LEN
    ahead = band_rows(filt_rows, TOK_DEV, win_rows, LEN)
    behind = band_rows(filt_rows, win_rows, TOK_DEV, 0)
    places = jnp.arange(SEQ, dtype=jnp.int32)
    local_rows = jnp.arange(TOK_DEV, dtype=jnp.int32)
    window_rows = jnp.arange(win_rows, dtype=jnp.int32)
    blocks = jnp.arange(SHARDS, dtype=jnp.int32)
    highest = lax.Precision.HIGHEST

    def one_window(pieces):
        proj_w, grad_w, starts_w = pieces
        latest = last_starts(starts_w)
        source = proj_w.astype(jnp.float32)
        featured = jnp.zeros((SEQ, 3 * C), jnp.float32)
        for offset in range(SHORT):
            shifted = jnp.concatenate([jnp.zeros((offset, 3 * C), jnp.float32), source[:SEQ - offset]], axis=0)
            featured = featured + short_taps[offset] * jnp.where((latest <= places - offset)[:, None], shifted, 0.0)
        query_feat = featured[:, :C]
        key_feat = featured[:, C:2 * C]
        value_feat = featured[:, 2 * C:]
        gating = rounded(key_feat * value_feat)
        gate_pad = jnp.concatenate([jnp.zeros((LEN, C), jnp.float32), gating], axis=0)

        def ahead_linked(first_row):
            own_latest = lax.dynamic_slice_in_dim(latest, first_row, TOK_DEV, 0)
            return own_latest[:, None] <= (first_row - LEN + window_rows)[None, :]

        def forward_block(block_id):
            first_row = block_id * TOK_DEV
            window = lax.dynamic_slice_in_dim(gate_pad, first_row, win_rows, 0).reshape(win_rows, GROUPS, GROUP)
            weights = jnp.where(ahead_linked(first_row)[None], ahead, 0.0)
            return jnp.einsum("gts,sgc->tgc", weights, window, precision=highest).reshape(TOK_DEV, C)

        long_out = lax.map(forward_block, blocks).reshape(SEQ, C)
        combined = long_out + skip * gating
        mixed_w = (query_feat * combined).astype(jnp.bfloat16)
        upstream = grad_w.astype(jnp.float32)
        grad_query = upstream * combined
        through = upstream * query_feat
        grad_long_in = rounded(through)
        grad_pad = jnp.concatenate([grad_long_in, jnp.zeros((LEN, C), jnp.float32)], axis=0)
        latest_pad = jnp.concatenate([latest, jnp.full((LEN,), SEQ, jnp.int32)])

        def backward_block(block_id):
            first_row = block_id * TOK_DEV
            sources = lax.dynamic_slice_in_dim(grad_pad, first_row, win_rows, 0).reshape(win_rows, GROUPS, GROUP)
            their = lax.dynamic_slice_in_dim(latest_pad, first_row, win_rows, 0)
            linked = their[:, None] <= (first_row + local_rows)[None, :]
            weights = jnp.where(linked[None], behind, 0.0)
            block_grad = jnp.einsum("gut,ugc->tgc", weights, sources, precision=highest).reshape(TOK_DEV, C)
            window = lax.dynamic_slice_in_dim(gate_pad, first_row, win_rows, 0).reshape(win_rows, GROUPS, GROUP)
            rows_blk = lax.dynamic_slice_in_dim(grad_long_in, first_row, TOK_DEV, 0).reshape(TOK_DEV, GROUPS, GROUP)
            product = jnp.einsum("tgc,sgc->gts", rows_blk, window, precision=highest)
            product = jnp.where(ahead_linked(first_row)[None], product, 0.0)
            return block_grad, lag_totals(product, TOK_DEV, win_rows)

        gate_parts, lag_parts = lax.map(backward_block, blocks)
        grad_gate = gate_parts.reshape(SEQ, C) + skip * through
        grad_feat = jnp.concatenate([grad_query, grad_gate * value_feat, grad_gate * key_feat], axis=1)
        feat_pad = jnp.concatenate([grad_feat, jnp.zeros((SHORT, 3 * C), jnp.float32)], axis=0)
        latest_short = jnp.concatenate([latest, jnp.full((SHORT,), SEQ, jnp.int32)])
        grad_source = jnp.zeros((SEQ, 3 * C), jnp.float32)
        short_parts = []
        for offset in range(SHORT):
            later = feat_pad[offset:offset + SEQ]
            their = latest_short[offset:offset + SEQ]
            grad_source = grad_source + short_taps[offset] * jnp.where((their <= places)[:, None], later, 0.0)
            earlier = jnp.concatenate([jnp.zeros((offset, 3 * C), jnp.float32), source[:SEQ - offset]], axis=0)
            earlier = jnp.where((latest <= places - offset)[:, None], earlier, 0.0)
            short_parts.append(jnp.sum(grad_feat * earlier, axis=0))
        return (mixed_w, grad_source.astype(jnp.bfloat16), jnp.stack(short_parts),
                jnp.sum(lag_parts, axis=0).T, jnp.sum(through * gating, axis=0))

    outputs = lax.map(one_window, (proj, grad_out, starts))
    scaling = float(WINDOWS * SEQ) ** -0.5
    return (outputs[0], outputs[1], jnp.sum(outputs[2], axis=0) * scaling,
            jnp.sum(outputs[3], axis=0) * scaling, jnp.sum(outputs[4], axis=0) * scaling)
```

```python
import functools

import jax
import jax.numpy as jnp
from jax import lax
from jax.experimental import pallas as pl
from jax.experimental.pallas import tpu as pltpu
from jax.sharding import PartitionSpec as P

C = 4096
GROUP = 16
LEN = 128
SHORT = 7
TOK = 128
TAIL = 16
LANES = 128
BLK = 512
SLABS = BLK // LANES
PER_SLAB = LANES // GROUP
BLOCKS = C // BLK
CHUNKS = ((0, 2), (2, 2), (4, 2), (6, 2))
FAR = 1 << 20
VMEM_LIMIT = 48 * 1024 * 1024

bf16 = jnp.bfloat16
f32 = jnp.float32


def ring(block, distance):
    count = lax.axis_size("ctx")
    return lax.ppermute(block, "ctx", [(i, (i + distance) % count) for i in range(count)])


def dot(a, b):
    return jnp.dot(a, b, preferred_element_type=f32)


def link_tables(listed):
    rows = jnp.arange(TOK, dtype=jnp.int32)
    usable = listed < TOK
    first = jnp.min(jnp.where(usable, listed, FAR))
    last = jnp.max(jnp.where(usable, listed, -FAR))
    latest = jnp.max(
        jnp.where(usable[None, :] & (listed[None, :] <= rows[:, None]), listed[None, :], -FAR), axis=1
    )
    t, s = rows[:, None], rows[None, :]
    own = (s <= t) & (latest[:, None] <= s)
    before = (s > t) & (t < first)
    own_t = (t <= s) & (latest[None, :] <= t)
    after_t = (t > s) & (t >= last)
    turned = s == TOK - 1 - t
    masks = jnp.stack([own, before, own_t, after_t, own[::-1], before[::-1], turned]).astype(bf16)
    lags = jnp.arange(1, SHORT, dtype=jnp.int32)[:, None, None]
    cols = jnp.arange(TAIL + TOK, dtype=jnp.int32)[None, None, :] - TAIL
    here = rows[None, :, None]
    shifts = (cols == here - lags) & (latest[None, :, None] <= here - lags)
    later = rows[None, None, :]
    unshifts = (later == here + lags) & (latest[None, None, :] <= here)
    shifts = shifts.astype(bf16).reshape((SHORT - 1) * TOK, TAIL + TOK)
    unshifts = unshifts.astype(bf16).reshape((SHORT - 1) * TOK, TOK)
    sends = jnp.stack([rows >= last, rows < first], axis=1).astype(f32)
    return masks, shifts, unshifts, sends, last, first


def short_sum(taps, near, moved):
    total = taps[0:1] * near
    for lag in range(1, SHORT):
        total = total + taps[lag : lag + 1] * moved[(lag - 1) * TOK : lag * TOK]
    return total


def feature_kernel(
    xq, xk, xv, tq, tk, tv, wq, wk, wv, grad_ref, shift_ref, send_ref,
    feat_ref, gate_ref, long_ref, gate_send_ref, long_send_ref,
):
    feats = []
    for place, (x, tail, taps) in enumerate(((xq, tq, wq), (xk, tk, wk), (xv, tv, wv))):
        own = x[...]
        moved = dot(shift_ref[...], jnp.concatenate([tail[...], own], axis=0))
        feat = short_sum(taps[0], own.astype(f32), moved)
        feat_ref[place] = feat
        feats.append(feat)
    gate = (feats[1] * feats[2]).astype(bf16)
    long_in = (grad_ref[...].astype(f32) * feats[0]).astype(bf16)
    gate_ref[...] = gate
    long_ref[...] = long_in
    gate_send_ref[...] = (gate.astype(f32) * send_ref[:, 0:1]).astype(bf16)
    long_send_ref[...] = (long_in.astype(f32) * send_ref[:, 1:2]).astype(bf16)


def feature_call(chunk, proj, tail, params, grad_out, shifts, sends, per_shard):
    base, count = chunk
    wide = count * BLK

    def cols(part):
        return lambda j: (0, part * BLOCKS + base + j)

    def taps(part):
        def index(j):
            place = part * BLOCKS + base + j
            return (place // per_shard, 0, place % per_shard)

        return index

    whole = lambda j: (0, 0)
    here = pl.BlockSpec((TOK, BLK), lambda j: (0, j))
    return pl.pallas_call(
        feature_kernel,
        grid=(count,),
        in_specs=[pl.BlockSpec((TOK, BLK), cols(part)) for part in range(3)]
        + [pl.BlockSpec((TAIL, BLK), cols(part)) for part in range(3)]
        + [pl.BlockSpec((1, 8, BLK), taps(part)) for part in range(3)]
        + [
            pl.BlockSpec((TOK, BLK), cols(0)),
            pl.BlockSpec(shifts.shape, whole),
            pl.BlockSpec(sends.shape, whole),
        ],
        out_specs=[pl.BlockSpec((3, TOK, BLK), lambda j: (0, 0, j)), here, here, here, here],
        out_shape=[jax.ShapeDtypeStruct((3, TOK, wide), f32)]
        + [jax.ShapeDtypeStruct((TOK, wide), bf16)] * 4,
        compiler_params=pltpu.CompilerParams(vmem_limit_bytes=VMEM_LIMIT),
        cost_estimate=pl.CostEstimate(
            flops=2 * 3 * 768 * 144 * wide, bytes_accessed=30 * TOK * wide, transcendentals=0
        ),
        name="features",
    )(proj, proj, proj, tail, tail, tail, params, params, params, grad_out, shifts, sends)


def main_kernel(
    feat_ref, gate_ref, long_ref, gate_halo_ref, long_halo_ref, grad_ref, x_ref, tail_ref, taps_ref,
    skip_ref, filt_ref, filt_back_ref, mask_ref, shift_ref, unshift_ref, send_ref, *rest,
):
    (mixed_ref, source_ref, short_ref, lag_ref, skip_grad_ref, head_ref, end_ref,
     ahead_ref, behind_ref, picked_ref, long_out_ref, gate_grad_ref, feat_grad_ref) = rest[-13:]
    part = pl.program_id(1)

    @pl.when(part == 0)
    def _():
        lane_group = lax.broadcasted_iota(jnp.int32, (TOK, LANES), 1) // GROUP

        def slab(step, carry):
            lanes = pl.ds(pl.multiple_of(step * LANES, LANES), LANES)
            gates = jnp.concatenate([gate_ref[:, lanes], gate_halo_ref[:, lanes]], axis=0)
            own_long = long_ref[:, lanes]
            longs = jnp.concatenate([own_long, long_halo_ref[:, lanes]], axis=0)
            turned = dot(mask_ref[6], own_long).astype(bf16)
            rows = pl.ds(pl.multiple_of(step * PER_SLAB, PER_SLAB), PER_SLAB)
            fore = filt_back_ref[rows, :]
            back = filt_ref[rows, :]
            for g in range(PER_SLAB):
                place = slice(g * TOK, (g + 1) * TOK)
                band = jnp.broadcast_to(fore[g : g + 1], (TOK, LANES))
                band = pltpu.roll(band, 0, 1, stride=1, stride_axis=0).astype(bf16)
                ahead_ref[place, :TOK] = band * mask_ref[0]
                ahead_ref[place, TOK:] = band * mask_ref[1]
                band = jnp.broadcast_to(back[g : g + 1], (TOK, LANES))
                band = pltpu.roll(band, 0, 1, stride=1, stride_axis=0).astype(bf16)
                behind_ref[place, :TOK] = band * mask_ref[2]
                behind_ref[place, TOK:] = band * mask_ref[3]
                picked_ref[place, :] = jnp.where(lane_group == g, turned, jnp.zeros_like(turned))
            forward = dot(ahead_ref[...], gates)
            backward = dot(behind_ref[...], longs)
            out = jnp.zeros((TOK, LANES), f32)
            spread = jnp.zeros((TOK, LANES), f32)
            for g in range(PER_SLAB):
                place = slice(g * TOK, (g + 1) * TOK)
                out = jnp.where(lane_group == g, forward[place], out)
                spread = jnp.where(lane_group == g, backward[place], spread)
            long_out_ref[:, lanes] = out
            gate_grad_ref[:, lanes] = spread
            product = lax.dot_general(
                picked_ref[...], gates, (((1,), (1,)), ((), ())), preferred_element_type=f32
            )
            own_mask = mask_ref[4].astype(f32)
            before_mask = mask_ref[5].astype(f32)
            sums = []
            for g in range(PER_SLAB):
                place = slice(g * TOK, (g + 1) * TOK)
                kept = product[place, :TOK] * own_mask + product[place, TOK:] * before_mask
                kept = pltpu.roll(kept, 0, 1, stride=1, stride_axis=0)
                sums.append(jnp.sum(kept, axis=0, keepdims=True))
            lag_ref[rows, :] = jnp.concatenate(sums, axis=0)
            return carry

        lax.fori_loop(0, SLABS, slab, 0)
        gate = gate_ref[...].astype(f32)
        upstream = grad_ref[...].astype(f32)
        query = feat_ref[0]
        skip = skip_ref[0, 7:8, :]
        combined = long_out_ref[...] + skip * gate
        through = upstream * query
        mixed_ref[...] = (query * combined).astype(bf16)
        feat_grad_ref[0] = upstream * combined
        gate_grad = gate_grad_ref[...] + skip * through
        feat_grad_ref[1] = gate_grad * feat_ref[2]
        feat_grad_ref[2] = gate_grad * feat_ref[1]
        skip_grad = jnp.sum(through * gate, axis=0, keepdims=True)
        for k in range(SLABS):
            skip_grad_ref[k] = skip_grad[:, k * LANES : (k + 1) * LANES]

    feat_grad = feat_grad_ref[part]
    own = x_ref[...]
    moved = dot(shift_ref[...], jnp.concatenate([tail_ref[...], own], axis=0))
    near = own.astype(f32)
    sums = [jnp.sum(feat_grad * near, axis=0, keepdims=True)]
    for lag in range(1, SHORT):
        sums.append(
            jnp.sum(feat_grad * moved[(lag - 1) * TOK : lag * TOK], axis=0, keepdims=True)
        )
    sums.append(jnp.zeros_like(sums[0]))
    sums = jnp.concatenate(sums, axis=0)
    for k in range(SLABS):
        short_ref[k] = sums[:, k * LANES : (k + 1) * LANES]
    source = short_sum(taps_ref[0], feat_grad, dot(unshift_ref[...], feat_grad.astype(bf16)))
    source_ref[...] = source.astype(bf16)
    end_ref[...] = source[TOK - 8 :]
    head_ref[...] = (feat_grad[:TAIL] * send_ref[:TAIL, 1:2]).astype(bf16)


def main_call(chunk, feats, gates, longs, gate_halo, long_halo, grad_out, proj, tail, params,
              filt, filt_back, masks, shifts, unshifts, sends, per_shard, kept):
    base, count = chunk
    shards = params.shape[0]
    skip_blocks = BLOCKS // shards
    local = pl.BlockSpec((TOK, BLK), lambda j, p: (0, j))
    first_cols = pl.BlockSpec((TOK, BLK), lambda j, p: (0, base + j))

    def cols(rows):
        return pl.BlockSpec((rows, BLK), lambda j, p: (0, p * BLOCKS + base + j))

    def taps(j, p):
        place = p * BLOCKS + base + j
        return (place // per_shard, 0, place % per_shard)

    def skips(j, p):
        return ((base + j) // skip_blocks, 0, (base + j) % skip_blocks)

    def whole(array):
        return pl.BlockSpec(array.shape, lambda j, p: (0,) * array.ndim)

    groups = BLK // GROUP
    filt_spec = pl.BlockSpec((groups, LEN), lambda j, p: (base + j, 0))
    operands = [feats, gates, longs, gate_halo, long_halo, grad_out, proj, tail, params, params,
                filt, filt_back, masks, shifts, unshifts, sends]
    in_specs = [
        pl.BlockSpec((3, TOK, BLK), lambda j, p: (0, 0, j)), local, local, local, local, first_cols,
        cols(TOK), cols(TAIL), pl.BlockSpec((1, 8, BLK), taps), pl.BlockSpec((1, 8, BLK), skips),
        filt_spec, filt_spec, whole(masks), whole(shifts), whole(unshifts), whole(sends),
    ]
    aliases = {}
    if kept is not None:
        aliases = {len(operands) + k: k for k in range(len(kept))}
        operands = operands + list(kept)
        in_specs = in_specs + [pl.BlockSpec(memory_space=pl.ANY)] * len(kept)
    slabs = C // LANES
    return pl.pallas_call(
        main_kernel,
        grid=(count, 3),
        in_specs=in_specs,
        out_specs=[
            first_cols, cols(TOK),
            pl.BlockSpec((SLABS, 8, LANES), lambda j, p: (p * BLOCKS + base + j, 0, 0)),
            pl.BlockSpec((groups, LANES), lambda j, p: (base + j, 0)),
            pl.BlockSpec((SLABS, 1, LANES), lambda j, p: (base + j, 0, 0)),
            cols(TAIL), cols(8),
        ],
        out_shape=[
            jax.ShapeDtypeStruct((TOK, C), bf16),
            jax.ShapeDtypeStruct((TOK, 3 * C), bf16),
            jax.ShapeDtypeStruct((3 * slabs, 8, LANES), f32),
            jax.ShapeDtypeStruct((C // GROUP, LANES), f32),
            jax.ShapeDtypeStruct((slabs, 1, LANES), f32),
            jax.ShapeDtypeStruct((TAIL, 3 * C), bf16),
            jax.ShapeDtypeStruct((8, 3 * C), f32),
        ],
        scratch_shapes=[
            pltpu.VMEM((PER_SLAB * TOK, 2 * TOK), bf16),
            pltpu.VMEM((PER_SLAB * TOK, 2 * TOK), bf16),
            pltpu.VMEM((PER_SLAB * TOK, LANES), bf16),
            pltpu.VMEM((TOK, BLK), f32),
            pltpu.VMEM((TOK, BLK), f32),
            pltpu.VMEM((3, TOK, BLK), f32),
        ],
        input_output_aliases=aliases,
        compiler_params=pltpu.CompilerParams(vmem_limit_bytes=VMEM_LIMIT),
        cost_estimate=pl.CostEstimate(
            flops=20_000_000_000 * count, bytes_accessed=40 * TOK * count * BLK, transcendentals=0
        ),
        name="main",
    )(*operands)


def patch_kernel(source_ref, end_ref, head_ref, taps_ref, keep_ref, out_ref):
    ahead = jnp.concatenate([jnp.zeros((8, head_ref.shape[1]), f32), head_ref[...].astype(f32)[:8]], axis=0)
    extra = jnp.zeros((8, head_ref.shape[1]), f32)
    taps = taps_ref[0]
    for lag in range(1, SHORT):
        extra = extra + taps[lag : lag + 1] * ahead[lag : lag + 8]
    final = end_ref[...] + extra * keep_ref[...]
    out_ref[...] = jnp.concatenate([source_ref[...].astype(f32)[:8], final], axis=0).astype(bf16)


def patch_call(source, end, head, params, keep):
    wide = params.shape[2]
    rows = TOK // TAIL - 1
    return pl.pallas_call(
        patch_kernel,
        grid=(3 * C // wide,),
        in_specs=[
            pl.BlockSpec((TAIL, wide), lambda j: (rows, j)),
            pl.BlockSpec((8, wide), lambda j: (0, j)),
            pl.BlockSpec((TAIL, wide), lambda j: (0, j)),
            pl.BlockSpec((1, 8, wide), lambda j: (j, 0, 0)),
            pl.BlockSpec((8, 1), lambda j: (0, 0)),
        ],
        out_specs=pl.BlockSpec((TAIL, wide), lambda j: (rows, j)),
        out_shape=jax.ShapeDtypeStruct(source.shape, bf16),
        input_output_aliases={0: 0},
        name="patch",
    )(source, end, head, params, keep)


def body(proj, short_taps, long_filter, skip, grad_out, starts):
    shards, count = lax.axis_size("fsdp"), lax.axis_size("ctx")
    source, upstream = proj[0], grad_out[0]
    masks, shifts, unshifts, sends, last, _ = link_tables(starts[0, 0])
    rows = jnp.arange(TOK - 8, TOK, dtype=jnp.int32)[:, None]
    tail = jnp.where(rows >= last, source[TOK - 8 :], jnp.zeros((), bf16))
    tail = jnp.pad(ring(tail, 1), ((TAIL - 8, 0), (0, 0)))
    wide = short_taps.shape[1]
    filt_rows = -(-long_filter.size // wide)
    flat = jnp.pad(long_filter.T.reshape(-1), (0, filt_rows * wide - long_filter.size))
    packed = jnp.concatenate(
        [short_taps, jnp.pad(skip, (0, wide - skip.shape[0]))[None], flat.reshape(filt_rows, wide)]
    )
    params = lax.all_to_all(
        jnp.broadcast_to(packed[None], (shards,) + packed.shape), "fsdp", 0, 0, tiled=True
    )
    filt = params[:, 8:].reshape(shards, -1)[:, : long_filter.size].reshape(C // GROUP, LEN)
    filt = filt.astype(bf16).astype(f32)
    filt_back = jnp.roll(filt[:, ::-1], 1, axis=1)
    per_shard = wide // BLK

    parts = []
    for chunk in CHUNKS:
        feats, gates, longs, gate_send, long_send = feature_call(
            chunk, source, tail, params, upstream, shifts, sends, per_shard
        )
        parts.append((feats, gates, longs, ring(gate_send, 1), ring(long_send, -1)))
    kept = None
    for chunk, part in zip(CHUNKS, parts):
        kept = main_call(
            chunk, *part, upstream, source, tail, params, filt, filt_back, masks, shifts, unshifts,
            sends, per_shard, kept,
        )
    mixed, grad_source, short_sums, lag_sums, skip_sums, head, end = kept
    head = ring(head, -1)

    short_sums = short_sums.reshape(shards, -1, 8, LANES)
    skip_slabs = C // LANES // shards
    short_sums = short_sums.at[:, :skip_slabs, 7].set(skip_sums.reshape(shards, skip_slabs, LANES))
    sums = jnp.concatenate(
        [short_sums.reshape(shards, -1, LANES), lag_sums.reshape(shards, -1, LANES)], axis=1
    )
    piece = sums.shape[1] // count
    sums = sums.reshape(shards * count, piece, LANES)
    sums = jnp.sum(lax.all_to_all(sums, ("fsdp", "ctx"), 0, 0, tiled=True), axis=0)
    sums = sums * (float(shards * count * TOK) ** -0.5)
    sums = lax.all_to_all(
        jnp.broadcast_to(sums[None], (count,) + sums.shape), "ctx", 0, 0, tiled=True
    ).reshape(count * piece, LANES)
    slabs = 3 * C // LANES // shards
    grad_short = sums[: slabs * 8].reshape(slabs, 8, LANES)
    grad_skip = grad_short[:skip_slabs, 7].reshape(-1)
    grad_short = grad_short[:, :SHORT].transpose(1, 0, 2).reshape(SHORT, -1)
    grad_long = sums[slabs * 8 :, ::-1].T

    keep = (rows >= last).astype(f32)
    grad_source = patch_call(grad_source, end, head, params, keep)
    return mixed[None], grad_source[None], grad_short, grad_long, grad_skip


def solution(mesh):
    placed = (
        P("fsdp", "ctx", None),
        P(None, "fsdp"),
        P(None, "fsdp"),
        P("fsdp"),
        P("fsdp", "ctx", None),
        P("fsdp", "ctx", None),
    )
    return jax.shard_map(
        body,
        mesh=mesh,
        in_specs=placed,
        out_specs=(
            P("fsdp", "ctx", None),
            P("fsdp", "ctx", None),
            P(None, "fsdp"),
            P(None, "fsdp"),
            P("fsdp"),
        ),
        check_vma=False,
    )
```

```python
import functools

import jax
import jax.numpy as jnp
from jax import lax
from jax.experimental import pallas as pl
from jax.experimental.pallas import tpu as pltpu
from jax.sharding import PartitionSpec as P

C = 4096
GROUP = 16
LEN = 128
SHORT = 7
TOK = 128
TAIL = 16
WIDE = TOK + TAIL
LANES = 128
BLK = 512
SLABS = BLK // LANES
PER_SLAB = LANES // GROUP
BLOCKS = C // BLK
UNROLL = 4
CHUNKS = ((0, 2), (2, 2), (4, 2), (6, 2))
PACK = 32
FAR = 1 << 20
VMEM_LIMIT = 48 * 1024 * 1024

bf16 = jnp.bfloat16
f32 = jnp.float32


def ring(block, distance):
    count = lax.axis_size("ctx")
    return lax.ppermute(block, "ctx", [(i, (i + distance) % count) for i in range(count)])


def dot(a, b):
    return jnp.dot(a, b, preferred_element_type=f32)


def in_hbm(array):
    return pltpu.with_memory_space_constraint(array, pltpu.HBM)


def latest_start(listed, places):
    latest = jnp.full(places.shape, -FAR, jnp.int32)
    for k in range(listed.shape[1]):
        start = listed[:, k : k + 1]
        latest = jnp.maximum(latest, jnp.where((start < TOK) & (start <= places), start, -FAR))
    return latest


def put(ref, place, linked):
    ref[place] = jnp.where(linked, 1.0, 0.0).astype(ref.dtype)


def bounds(listed):
    usable = listed < TOK
    first = jnp.min(jnp.where(usable, listed, FAR), axis=1, keepdims=True)
    last = jnp.max(jnp.where(usable, listed, -FAR), axis=1, keepdims=True)
    return first, last


def shift_kernel(starts_ref, shift_ref, send_ref):
    listed = starts_ref[...]
    first, last = bounds(listed)
    here = lax.broadcasted_iota(jnp.int32, (TOK, WIDE), 0)
    cols = lax.broadcasted_iota(jnp.int32, (TOK, WIDE), 1)
    cols = jnp.where(cols < TOK, cols, jnp.where(cols < TOK + SHORT - 1, cols - (TOK + SHORT - 1), FAR))
    latest_here = latest_start(listed, here)
    for lag in range(1, SHORT):
        place = slice((lag - 1) * TOK, lag * TOK)
        put(shift_ref, place, (cols == here - lag) & (latest_here <= here - lag))
    side = lax.broadcasted_iota(jnp.int32, (TOK, 2), 1)
    rows = lax.broadcasted_iota(jnp.int32, (TOK, 2), 0)
    put(send_ref, slice(0, TOK), jnp.where(side == 0, rows - last, first - 1 - rows) >= 0)


def link_kernel(starts_ref, mask_ref, unshift_ref):
    listed = starts_ref[...]
    first, last = bounds(listed)
    t = lax.broadcasted_iota(jnp.int32, (TOK, TOK), 0)
    s = lax.broadcasted_iota(jnp.int32, (TOK, TOK), 1)
    back = TOK - 1 - t
    latest_t, latest_s = latest_start(listed, t), latest_start(listed, s)
    put(mask_ref, 0, (s <= t) & (latest_t <= s))
    put(mask_ref, 1, (s > t) & (t < first))
    put(mask_ref, 2, (t <= s) & (latest_s <= t))
    put(mask_ref, 3, (t > s) & (t >= last))
    put(mask_ref, 4, (s <= back) & (latest_start(listed, back) <= s))
    put(mask_ref, 5, (s > back) & (back < first))
    put(mask_ref, 6, s == back)
    put(mask_ref, 7, (s + t == TOK) | (s + t == 0))
    rows = lax.broadcasted_iota(jnp.int32, (TAIL, TOK), 0)
    tail = jnp.where(rows < SHORT - 1, rows - (SHORT - 1), FAR)
    later = lax.broadcasted_iota(jnp.int32, (TAIL, TOK), 1)
    latest_later = latest_start(listed, later)
    for lag in range(1, SHORT):
        first_row = (lag - 1) * WIDE
        put(unshift_ref, slice(first_row, first_row + TOK), (s == t + lag) & (latest_s <= t))
        linked = (later == tail + lag) & (latest_later <= tail)
        put(unshift_ref, slice(first_row + TOK, first_row + WIDE), linked)


def table_call(kernel, shapes, starts, name):
    return pl.pallas_call(
        kernel,
        in_specs=[pl.BlockSpec(memory_space=pltpu.VMEM)],
        out_specs=[pl.BlockSpec(memory_space=pltpu.VMEM)] * 2,
        out_shape=[jax.ShapeDtypeStruct(shape, dtype) for shape, dtype in shapes],
        cost_estimate=pl.CostEstimate(flops=5_000_000, bytes_accessed=1_000_000, transcendentals=0),
        name=name,
    )(starts)


def shift_call(starts):
    shapes = [(((SHORT - 1) * TOK, WIDE), bf16), ((TOK, 2), f32)]
    return table_call(shift_kernel, shapes, starts, "shifts")


def link_call(starts):
    shapes = [((8, TOK, TOK), bf16), (((SHORT - 1) * WIDE, TOK), bf16)]
    return table_call(link_kernel, shapes, starts, "links")


def short_sum(taps, near, moved, step):
    total = taps[0:1] * near
    for lag in range(1, SHORT):
        first = (lag - 1) * step
        total = total + taps[lag : lag + 1] * moved[first : first + TOK]
    return total


def tap_rows(packed):
    return jnp.concatenate([packed[0, 8 * k : 8 * k + 8] for k in range(SLABS)], axis=1)


def tail_rows(tail):
    tail = tail[...].astype(f32)
    empty = jnp.zeros((TAIL - tail.shape[0], tail.shape[1]), f32)
    return jnp.concatenate([tail, empty], axis=0).astype(bf16)


def feature_kernel(
    xq, xk, xv, tq, tk, tv, wq, wk, wv, grad_ref, shift_ref, send_ref,
    gate_send_ref, long_send_ref, feat_ref,
):
    feats = []
    for part, (x, tail, taps) in enumerate(((xq, tq, wq), (xk, tk, wk), (xv, tv, wv))):
        own = x[...]
        moved = dot(shift_ref[...], jnp.concatenate([own, tail_rows(tail)], axis=0))
        feats.append(short_sum(tap_rows(taps), own.astype(f32), moved, TOK))
        feat_ref[part] = feats[part]
    gate = (feats[1] * feats[2]).astype(bf16)
    long_in = (grad_ref[...].astype(f32) * feats[0]).astype(bf16)
    gate_send_ref[...] = (gate.astype(f32) * send_ref[:, 0:1]).astype(bf16)
    long_send_ref[...] = (long_in.astype(f32) * send_ref[:, 1:2]).astype(bf16)


def feature_call(chunk, proj, tail, params, grad_out, shifts, sends, per_shard):
    base, count = chunk
    wide = count * BLK

    def cols(part):
        return lambda j: (0, part * BLOCKS + base + j)

    def taps(part):
        def index(j):
            place = part * BLOCKS + base + j
            return (place // per_shard, place % per_shard, 0)

        return index

    whole = lambda j: (0, 0)
    here = pl.BlockSpec((TOK, BLK), lambda j: (0, j))
    return pl.pallas_call(
        feature_kernel,
        grid=(count,),
        in_specs=[pl.BlockSpec((TOK, BLK), cols(part)) for part in range(3)]
        + [pl.BlockSpec((SHORT - 1, BLK), cols(part)) for part in range(3)]
        + [pl.BlockSpec((1, PACK, LANES), taps(part)) for part in range(3)]
        + [
            pl.BlockSpec((TOK, BLK), cols(0)),
            pl.BlockSpec(shifts.shape, whole),
            pl.BlockSpec(sends.shape, whole),
        ],
        out_specs=[here, here, pl.BlockSpec((3, TOK, BLK), lambda j: (0, 0, j))],
        out_shape=[jax.ShapeDtypeStruct((TOK, wide), bf16)] * 2 + [pltpu.HBM((3, TOK, wide), f32)],
        compiler_params=pltpu.CompilerParams(vmem_limit_bytes=VMEM_LIMIT),
        cost_estimate=pl.CostEstimate(
            flops=2 * 3 * 768 * 144 * wide, bytes_accessed=12 * TOK * wide, transcendentals=0
        ),
        name="features",
    )(*[in_hbm(proj)] * 3, tail, tail, tail, params, params, params, in_hbm(grad_out), in_hbm(shifts), in_hbm(sends))


def main_kernel(
    gate_halo_ref, long_halo_ref, feat_ref, grad_ref, xq, xk, xv, tq, tk, tv, wq, wk, wv,
    skip_ref, filt_ref, mask_ref, unshift_ref, send_ref, *rest,
):
    (mixed_ref, source_ref, short_ref, lag_ref, skip_grad_ref, head_ref, end_ref,
     gate_ref, long_ref, long_out_ref, gate_grad_ref, feat_grad_ref, padded_ref,
     taps_ref, fore_ref, back_ref, ready_ref, sems) = rest[-18:]
    base = rest[0]
    count, step = pl.num_programs(0), pl.program_id(0)
    lane_group = lax.broadcasted_iota(jnp.int32, (TOK, LANES), 1) // GROUP

    def copies(at):
        slot = at % 2
        return [
            pltpu.make_async_copy(
                ready_ref.at[slot, part],
                source_ref.at[:, pl.ds(pl.multiple_of((part * BLOCKS + base + at) * BLK, BLK), BLK)],
                sems.at[slot, part],
            )
            for part in range(3)
        ]

    for part, (x, tail, taps) in enumerate(((xq, tq, wq), (xk, tk, wk), (xv, tv, wv))):
        padded_ref[part, :TOK] = x[...]
        padded_ref[part, TOK:] = tail_rows(tail)
        taps_ref[part] = tap_rows(taps)

    filt = filt_ref[0].astype(bf16)
    back_ref[...] = filt.astype(f32)
    fore_ref[...] = dot(filt, mask_ref[7])

    gate_ref[...] = (feat_ref[1] * feat_ref[2]).astype(bf16)
    long_ref[...] = (grad_ref[...].astype(f32) * feat_ref[0]).astype(bf16)

    def slab(at, carry):
        lanes = pl.ds(pl.multiple_of(at * LANES, LANES), LANES)
        own_long = long_ref[:, lanes]
        gates = jnp.concatenate([gate_ref[:, lanes], gate_halo_ref[:, lanes]], axis=0)
        longs = jnp.concatenate([own_long, long_halo_ref[:, lanes]], axis=0)
        turned = dot(mask_ref[6], own_long).astype(bf16)
        rows = pl.ds(pl.multiple_of(at * PER_SLAB, PER_SLAB), PER_SLAB)
        fore = fore_ref[rows, :]
        back = back_ref[rows, :]
        own_mask = mask_ref[4].astype(f32)
        before_mask = mask_ref[5].astype(f32)
        def bands(rows_of, first, second):
            made = []
            for g in range(PER_SLAB):
                band = jnp.broadcast_to(rows_of[g : g + 1], (TOK, LANES))
                band = pltpu.roll(band, 0, 1, stride=1, stride_axis=0).astype(bf16)
                made.append(jnp.concatenate([band * first, band * second], axis=1))
            return jnp.concatenate(made, axis=0)

        def gathered(wide):
            total = wide[:TOK]
            for g in range(1, PER_SLAB):
                total = jnp.where(lane_group == g, wide[g * TOK : (g + 1) * TOK], total)
            return total

        out = gathered(dot(bands(fore, mask_ref[0], mask_ref[1]), gates))
        spread = gathered(dot(bands(back, mask_ref[2], mask_ref[3]), longs))
        picked = jnp.concatenate(
            [jnp.where(lane_group == g, turned, jnp.zeros_like(turned)) for g in range(PER_SLAB)], axis=0
        )
        product = lax.dot_general(picked, gates, (((1,), (1,)), ((), ())), preferred_element_type=f32)
        sums = []
        for g in range(PER_SLAB):
            place = slice(g * TOK, (g + 1) * TOK)
            kept = product[place, :TOK] * own_mask + product[place, TOK:] * before_mask
            kept = pltpu.roll(kept, 0, 1, stride=1, stride_axis=0)
            sums.append(jnp.sum(kept, axis=0, keepdims=True))
        long_out_ref[:, lanes] = out
        gate_grad_ref[:, lanes] = spread
        lag_ref[rows, :] = jnp.concatenate(sums, axis=0)
        return carry

    lax.fori_loop(0, SLABS, slab, 0, unroll=UNROLL)
    gate = gate_ref[...].astype(f32)
    upstream = grad_ref[...].astype(f32)
    query = feat_ref[0]
    skip = tap_rows(skip_ref)[7:8]
    combined = long_out_ref[...] + skip * gate
    through = upstream * query
    mixed_ref[...] = (query * combined).astype(bf16)
    feat_grad_ref[0] = upstream * combined
    gate_grad = gate_grad_ref[...] + skip * through
    feat_grad_ref[1] = gate_grad * feat_ref[2]
    feat_grad_ref[2] = gate_grad * feat_ref[1]
    skip_grad = jnp.sum(through * gate, axis=0, keepdims=True)
    for k in range(SLABS):
        skip_grad_ref[k] = skip_grad[:, k * LANES : (k + 1) * LANES]

    @pl.when(step >= 2)
    def _():
        for copy in copies(step - 2):
            copy.wait()

    def column_part(part, carry):
        feat_grad = feat_grad_ref[part]
        moved = dot(unshift_ref[...], feat_grad.astype(bf16))
        near = padded_ref[part, :TOK].astype(f32)
        tail = padded_ref[part, TOK:].astype(f32)
        sums = [jnp.sum(near * feat_grad, axis=0, keepdims=True)]
        for lag in range(1, SHORT):
            first = (lag - 1) * WIDE
            own = jnp.sum(near * moved[first : first + TOK], axis=0, keepdims=True)
            before = jnp.sum(tail * moved[first + TOK : first + WIDE], axis=0, keepdims=True)
            sums.append(own + before)
        sums.append(jnp.zeros_like(sums[0]))
        sums = jnp.concatenate(sums, axis=0)
        for k in range(SLABS):
            short_ref[part, k] = sums[:, k * LANES : (k + 1) * LANES]
        source = short_sum(taps_ref[part], feat_grad, moved, WIDE)
        ready_ref[step % 2, part] = source.astype(bf16)
        end_ref[part] = source[TOK - 8 :]
        head_ref[part] = (feat_grad[:TAIL] * send_ref[:TAIL, 1:2]).astype(bf16)
        return carry

    lax.fori_loop(0, 3, column_part, 0)
    for copy in copies(step):
        copy.start()

    @pl.when(step == count - 1)
    def _():
        @pl.when(count >= 2)
        def _():
            for copy in copies(step - 1):
                copy.wait()

        for copy in copies(step):
            copy.wait()


def main_call(chunk, gate_halo, long_halo, feats, grad_out, proj, tail, params,
              masks, unshifts, sends, per_shard, kept):
    base, count = chunk
    shards = params.shape[0]
    own_blocks = BLOCKS // shards
    local = pl.BlockSpec((TOK, BLK), lambda j: (0, j))
    first_cols = pl.BlockSpec((TOK, BLK), lambda j: (0, base + j))

    def cols(rows, part):
        return pl.BlockSpec((rows, BLK), lambda j: (0, part * BLOCKS + base + j))

    def taps(part):
        def index(j):
            place = part * BLOCKS + base + j
            return (place // per_shard, place % per_shard, 0)

        return pl.BlockSpec((1, PACK, LANES), index)

    def skips(j):
        return ((base + j) // own_blocks, (base + j) % own_blocks, 0)

    def filters(j):
        return ((base + j) // own_blocks, per_shard + (base + j) % own_blocks, 0)

    def whole(array):
        return pl.BlockSpec(array.shape, lambda j: (0,) * array.ndim)

    groups = BLK // GROUP
    operands = [gate_halo, long_halo, feats, in_hbm(grad_out), *[in_hbm(proj)] * 3, tail, tail, tail,
                params, params, params, params, params, *[in_hbm(table) for table in (masks, unshifts, sends)]]
    in_specs = (
        [local, local, pl.BlockSpec((3, TOK, BLK), lambda j: (0, 0, j)), first_cols]
        + [cols(TOK, part) for part in range(3)]
        + [cols(SHORT - 1, part) for part in range(3)]
        + [taps(part) for part in range(3)]
        + [pl.BlockSpec((1, PACK, LANES), skips), pl.BlockSpec((1, PACK, LANES), filters)]
        + [whole(masks), whole(unshifts), whole(sends)]
    )
    aliases = {}
    if kept is not None:
        aliases = {len(operands) + k: k for k in range(len(kept))}
        operands = operands + list(kept)
        in_specs = in_specs + [pl.BlockSpec(memory_space=pl.ANY)] * len(kept)
    slabs = C // LANES
    places = len(operands) - (0 if kept is None else len(kept))

    def kernel(*refs):
        main_kernel(*refs[:places], base, *refs[places:])

    return pl.pallas_call(
        kernel,
        grid=(count,),
        in_specs=in_specs,
        out_specs=[
            first_cols,
            pl.BlockSpec(memory_space=pl.ANY),
            pl.BlockSpec((3, SLABS, 8, LANES), lambda j: (0, base + j, 0, 0)),
            pl.BlockSpec((groups, LANES), lambda j: (base + j, 0)),
            pl.BlockSpec((SLABS, 1, LANES), lambda j: (base + j, 0, 0)),
            pl.BlockSpec((3, TAIL, BLK), lambda j: (0, 0, base + j)),
            pl.BlockSpec((3, 8, BLK), lambda j: (0, 0, base + j)),
        ],
        out_shape=[
            jax.ShapeDtypeStruct((TOK, C), bf16),
            jax.ShapeDtypeStruct((TOK, 3 * C), bf16),
            jax.ShapeDtypeStruct((3, slabs, 8, LANES), f32),
            jax.ShapeDtypeStruct((C // GROUP, LANES), f32),
            jax.ShapeDtypeStruct((slabs, 1, LANES), f32),
            jax.ShapeDtypeStruct((3, TAIL, C), bf16),
            jax.ShapeDtypeStruct((3, 8, C), f32),
        ],
        scratch_shapes=[
            pltpu.VMEM((TOK, BLK), bf16),
            pltpu.VMEM((TOK, BLK), bf16),
            pltpu.VMEM((TOK, BLK), f32),
            pltpu.VMEM((TOK, BLK), f32),
            pltpu.VMEM((3, TOK, BLK), f32),
            pltpu.VMEM((3, TOK + TAIL, BLK), bf16),
            pltpu.VMEM((3, 8, BLK), f32),
            pltpu.VMEM((PACK, LANES), f32),
            pltpu.VMEM((PACK, LANES), f32),
            pltpu.VMEM((2, 3, TOK, BLK), bf16),
            pltpu.SemaphoreType.DMA((2, 3)),
        ],
        input_output_aliases=aliases,
        compiler_params=pltpu.CompilerParams(vmem_limit_bytes=VMEM_LIMIT),
        cost_estimate=pl.CostEstimate(
            flops=5_000_000_000 * count, bytes_accessed=40 * TOK * count * BLK, transcendentals=0
        ),
        name="main",
    )(*operands)


def patch_kernel(starts_ref, source_ref, end_ref, head_ref, params_ref, out_ref):
    rows = lax.broadcasted_iota(jnp.int32, (8, BLK), 0) + (TOK - 8)
    listed = starts_ref[...]
    last = jnp.max(jnp.where(listed < TOK, listed, -FAR), axis=1, keepdims=True)
    keep = jnp.where(rows >= last, 1.0, 0.0)
    shards = params_ref.shape[0]
    per_shard = 3 * BLOCKS // shards
    for place in range(3 * BLOCKS):
        part, first = place // BLOCKS, place % BLOCKS * BLK
        own = slice(first, first + BLK)
        head = head_ref[part, :, own].astype(f32)
        ahead = jnp.concatenate([jnp.zeros_like(head), head], axis=0)
        first = place % per_shard * PACK
        taps = tap_rows(params_ref[pl.ds(place // per_shard, 1), first : first + PACK])
        extra = jnp.zeros_like(head)
        for lag in range(1, SHORT):
            extra = extra + taps[lag : lag + 1] * ahead[lag : lag + 8]
        final = end_ref[part, :, own] + extra * keep
        lanes = slice(place * BLK, (place + 1) * BLK)
        before = source_ref[:, lanes].astype(f32)[:8]
        out_ref[:, lanes] = jnp.concatenate([before, final], axis=0).astype(bf16)


def patch_call(starts, source, end, head, params):
    rows = TOK // TAIL - 1

    def whole(array):
        return pl.BlockSpec(array.shape, lambda j: (0,) * array.ndim)

    strip = pl.BlockSpec((TAIL, 3 * C), lambda j: (rows, 0))
    return pl.pallas_call(
        patch_kernel,
        grid=(1,),
        in_specs=[whole(starts), strip, whole(end), whole(head), whole(params)],
        out_specs=strip,
        out_shape=jax.ShapeDtypeStruct(source.shape, bf16),
        input_output_aliases={1: 0},
        compiler_params=pltpu.CompilerParams(vmem_limit_bytes=VMEM_LIMIT),
        cost_estimate=pl.CostEstimate(flops=1_000_000, bytes_accessed=2_000_000, transcendentals=0),
        name="patch",
    )(starts, source, end, head, params)


def prepare_kernel(starts_hbm, source_hbm, taps_hbm, skip_hbm, filt_hbm, tail_ref, packed_ref,
                   starts_ref, source_ref, taps_ref, skip_ref, filt_ref, sems):
    copies = [
        pltpu.make_async_copy(starts_hbm, starts_ref, sems.at[0]),
        pltpu.make_async_copy(source_hbm.at[pl.ds(TOK - TAIL, TAIL), :], source_ref, sems.at[1]),
        pltpu.make_async_copy(taps_hbm, taps_ref, sems.at[2]),
        pltpu.make_async_copy(skip_hbm, skip_ref, sems.at[3]),
        pltpu.make_async_copy(filt_hbm, filt_ref, sems.at[4]),
    ]
    for copy in copies:
        copy.start()
    for copy in copies:
        copy.wait()
    listed = starts_ref[...]
    last = jnp.max(jnp.where(listed < TOK, listed, -FAR), axis=1, keepdims=True)
    rows = lax.broadcasted_iota(jnp.int32, (SHORT - 1, 1), 0) + (TOK - SHORT + 1)
    tail = source_ref[...].astype(f32)[TAIL - SHORT + 1 :]
    tail_ref[...] = (tail * jnp.where(rows >= last, 1.0, 0.0)).astype(bf16)
    own, slabs = skip_ref.shape[1], taps_ref.shape[1] // LANES
    empty = jnp.zeros((1, LANES), f32)
    rows = []
    for k in range(slabs):
        lanes = slice(k * LANES, (k + 1) * LANES)
        rows += [taps_ref[:, lanes], skip_ref[:, lanes] if k * LANES < own else empty]
    packed = jnp.concatenate(rows + [filt_ref[...]], axis=0)
    packed_ref[...] = packed


def prepare_call(starts, source, short_taps, skip, filt, shards):
    own = skip.shape[0]
    rows = short_taps.shape[1] // LANES * 8 + filt.shape[0]
    return pl.pallas_call(
        prepare_kernel,
        in_specs=[pl.BlockSpec(memory_space=pltpu.HBM)] * 5,
        out_specs=[pl.BlockSpec(memory_space=pltpu.VMEM)] * 2,
        out_shape=[
            jax.ShapeDtypeStruct((SHORT - 1, 3 * C), bf16),
            jax.ShapeDtypeStruct((rows, LANES), f32),
        ],
        scratch_shapes=[
            pltpu.VMEM(starts.shape, jnp.int32),
            pltpu.VMEM((TAIL, 3 * C), bf16),
            pltpu.VMEM(short_taps.shape, f32),
            pltpu.VMEM((1, own), f32),
            pltpu.VMEM(filt.shape, f32),
            pltpu.SemaphoreType.DMA((5,)),
        ],
        compiler_params=pltpu.CompilerParams(vmem_limit_bytes=VMEM_LIMIT),
        cost_estimate=pl.CostEstimate(flops=1_000_000, bytes_accessed=2_000_000, transcendentals=0),
        name="prepare",
    )(*[in_hbm(array) for array in (starts, source, short_taps, skip[None], filt)])


def body(proj, short_taps, long_filter, skip, grad_out, starts):
    shards, count = lax.axis_size("fsdp"), lax.axis_size("ctx")
    source, upstream = proj[0], grad_out[0]
    shifts, sends = shift_call(starts[0])
    masks, unshifts = link_call(starts[0])
    wide = short_taps.shape[1]
    per_shard = wide // BLK
    tail, packed = prepare_call(starts[0], source, short_taps, skip, long_filter.T, shards)
    tail = ring(tail, 1)
    params = lax.all_gather(packed, "fsdp", axis=0)
    parts = []
    for chunk in CHUNKS:
        gate_send, long_send, feats = feature_call(
            chunk, source, tail, params, upstream, shifts, sends, per_shard
        )
        parts.append((ring(gate_send, 1), ring(long_send, -1), feats))
    kept = None
    for chunk, part in zip(CHUNKS, parts):
        kept = main_call(
            chunk, *part, upstream, source, tail, params, masks, unshifts,
            sends, per_shard, kept,
        )
    mixed, grad_source, short_sums, lag_sums, skip_sums, head, end = kept
    head = ring(head[:, :8], -1)

    skip_slabs = C // LANES // shards
    skip_sums = skip_sums.reshape(shards, skip_slabs, 1, LANES)
    short_sums = short_sums.reshape(shards, -1, 8, LANES)
    room = ((0, 0), (0, short_sums.shape[1] - skip_slabs), (7, 0), (0, 0))
    short_sums = short_sums + jnp.pad(skip_sums, room)
    sums = jnp.concatenate(
        [short_sums.reshape(shards, -1, LANES), lag_sums.reshape(shards, -1, LANES)], axis=1
    )
    piece = sums.shape[1] // count
    sums = sums.reshape(shards * count, piece, LANES)
    sums = jnp.sum(lax.all_to_all(sums, ("fsdp", "ctx"), 0, 0, tiled=True), axis=0)
    sums = sums * (float(shards * count * TOK) ** -0.5)
    grad_source = patch_call(starts[0], grad_source, end, head, params)
    sums = lax.all_to_all(
        jnp.broadcast_to(sums[None], (count,) + sums.shape), "ctx", 0, 0, tiled=True
    ).reshape(count * piece, LANES)
    slabs = 3 * C // LANES // shards
    grad_short = sums[: slabs * 8].reshape(slabs, 8, LANES)
    grad_skip = grad_short[:skip_slabs, 7].reshape(-1)
    grad_short = grad_short[:, :SHORT].transpose(1, 0, 2).reshape(SHORT, -1)
    grad_long = sums[slabs * 8 :, ::-1].T
    return mixed[None], grad_source[None], grad_short, grad_long, grad_skip


def solution(mesh):
    placed = (
        P("fsdp", "ctx", None),
        P(None, "fsdp"),
        P(None, "fsdp"),
        P("fsdp"),
        P("fsdp", "ctx", None),
        P("fsdp", "ctx", None),
    )
    return jax.shard_map(
        body,
        mesh=mesh,
        in_specs=placed,
        out_specs=(
            P("fsdp", "ctx", None),
            P("fsdp", "ctx", None),
            P(None, "fsdp"),
            P(None, "fsdp"),
            P("fsdp"),
        ),
        check_vma=False,
    )
```

```python
import functools

import jax
import jax.numpy as jnp
from jax import lax
from jax.experimental import pallas as pl
from jax.experimental.pallas import tpu as pltpu
from jax.sharding import PartitionSpec as P

C = 4096
GROUP = 16
LEN = 128
SHORT = 7
TOK = 128
TAIL = 16
WIDE = TOK + TAIL
LANES = 128
BLK = 512
SLABS = BLK // LANES
PER_SLAB = LANES // GROUP
BLOCKS = C // BLK
UNROLL = 4
CHUNKS = ((0, 2), (2, 2), (4, 2), (6, 2))
PACK = 32
FAR = 1 << 20
VMEM_LIMIT = 48 * 1024 * 1024

bf16 = jnp.bfloat16
f32 = jnp.float32


def ring(block, distance):
    count = lax.axis_size("ctx")
    return lax.ppermute(block, "ctx", [(i, (i + distance) % count) for i in range(count)])


def dot(a, b):
    return jnp.dot(a, b, preferred_element_type=f32)


def in_hbm(array):
    return pltpu.with_memory_space_constraint(array, pltpu.HBM)


def latest_start(listed, places):
    latest = jnp.full(places.shape, -FAR, jnp.int32)
    for k in range(listed.shape[1]):
        start = listed[:, k : k + 1]
        latest = jnp.maximum(latest, jnp.where((start < TOK) & (start <= places), start, -FAR))
    return latest


def put(ref, place, linked):
    ref[place] = jnp.where(linked, 1.0, 0.0).astype(ref.dtype)


def bounds(listed):
    usable = listed < TOK
    first = jnp.min(jnp.where(usable, listed, FAR), axis=1, keepdims=True)
    last = jnp.max(jnp.where(usable, listed, -FAR), axis=1, keepdims=True)
    return first, last


def shift_kernel(starts_ref, shift_ref, send_ref):
    listed = starts_ref[...]
    first, last = bounds(listed)
    here = lax.broadcasted_iota(jnp.int32, (TOK, WIDE), 0)
    cols = lax.broadcasted_iota(jnp.int32, (TOK, WIDE), 1)
    cols = jnp.where(cols < TOK, cols, jnp.where(cols < TOK + SHORT - 1, cols - (TOK + SHORT - 1), FAR))
    latest_here = latest_start(listed, here)
    for lag in range(1, SHORT):
        place = slice((lag - 1) * TOK, lag * TOK)
        put(shift_ref, place, (cols == here - lag) & (latest_here <= here - lag))
    side = lax.broadcasted_iota(jnp.int32, (TOK, 2), 1)
    rows = lax.broadcasted_iota(jnp.int32, (TOK, 2), 0)
    put(send_ref, slice(0, TOK), jnp.where(side == 0, rows - last, first - 1 - rows) >= 0)


def link_kernel(starts_ref, mask_ref, unshift_ref):
    listed = starts_ref[...]
    first, last = bounds(listed)
    t = lax.broadcasted_iota(jnp.int32, (TOK, TOK), 0)
    s = lax.broadcasted_iota(jnp.int32, (TOK, TOK), 1)
    back = TOK - 1 - t
    latest_t, latest_s = latest_start(listed, t), latest_start(listed, s)
    put(mask_ref, 0, (s <= t) & (latest_t <= s))
    put(mask_ref, 1, (s > t) & (t < first))
    put(mask_ref, 2, (t <= s) & (latest_s <= t))
    put(mask_ref, 3, (t > s) & (t >= last))
    put(mask_ref, 4, (s <= back) & (latest_start(listed, back) <= s))
    put(mask_ref, 5, (s > back) & (back < first))
    put(mask_ref, 6, s == back)
    put(mask_ref, 7, (s + t == TOK) | (s + t == 0))
    rows = lax.broadcasted_iota(jnp.int32, (TAIL, TOK), 0)
    tail = jnp.where(rows < SHORT - 1, rows - (SHORT - 1), FAR)
    later = lax.broadcasted_iota(jnp.int32, (TAIL, TOK), 1)
    latest_later = latest_start(listed, later)
    for lag in range(1, SHORT):
        first_row = (lag - 1) * WIDE
        put(unshift_ref, slice(first_row, first_row + TOK), (s == t + lag) & (latest_s <= t))
        linked = (later == tail + lag) & (latest_later <= tail)
        put(unshift_ref, slice(first_row + TOK, first_row + WIDE), linked)


def table_call(kernel, shapes, starts, name):
    return pl.pallas_call(
        kernel,
        in_specs=[pl.BlockSpec(memory_space=pltpu.VMEM)],
        out_specs=[pl.BlockSpec(memory_space=pltpu.VMEM)] * 2,
        out_shape=[jax.ShapeDtypeStruct(shape, dtype) for shape, dtype in shapes],
        cost_estimate=pl.CostEstimate(flops=5_000_000, bytes_accessed=1_000_000, transcendentals=0),
        name=name,
    )(starts)


def shift_call(starts):
    shapes = [(((SHORT - 1) * TOK, WIDE), bf16), ((TOK, 2), f32)]
    return table_call(shift_kernel, shapes, starts, "shifts")


def link_call(starts):
    shapes = [((8, TOK, TOK), bf16), (((SHORT - 1) * WIDE, TOK), bf16)]
    return table_call(link_kernel, shapes, starts, "links")


def short_sum(taps, near, moved, step):
    total = taps[0:1] * near
    for lag in range(1, SHORT):
        first = (lag - 1) * step
        total = total + taps[lag : lag + 1] * moved[first : first + TOK]
    return total


def tap_rows(packed):
    return jnp.concatenate([packed[0, 8 * k : 8 * k + 8] for k in range(SLABS)], axis=1)


def tail_rows(tail):
    tail = tail[...].astype(f32)
    empty = jnp.zeros((TAIL - tail.shape[0], tail.shape[1]), f32)
    return jnp.concatenate([tail, empty], axis=0).astype(bf16)


def feature_kernel(
    xq, xk, xv, tq, tk, tv, wq, wk, wv, grad_ref, shift_ref, send_ref,
    gate_send_ref, long_send_ref, feat_ref,
):
    feats = []
    for part, (x, tail, taps) in enumerate(((xq, tq, wq), (xk, tk, wk), (xv, tv, wv))):
        own = x[...]
        moved = dot(shift_ref[...], jnp.concatenate([own, tail_rows(tail)], axis=0))
        feats.append(short_sum(tap_rows(taps), own.astype(f32), moved, TOK))
        feat_ref[part] = feats[part]
    gate = (feats[1] * feats[2]).astype(bf16)
    long_in = (grad_ref[...].astype(f32) * feats[0]).astype(bf16)
    gate_send_ref[...] = (gate.astype(f32) * send_ref[:, 0:1]).astype(bf16)
    long_send_ref[...] = (long_in.astype(f32) * send_ref[:, 1:2]).astype(bf16)


def feature_call(chunk, proj, tail, params, grad_out, shifts, sends, per_shard):
    base, count = chunk
    wide = count * BLK

    def cols(part):
        return lambda j: (0, part * BLOCKS + base + j)

    def taps(part):
        def index(j):
            place = part * BLOCKS + base + j
            return (place // per_shard, place % per_shard, 0)

        return index

    whole = lambda j: (0, 0)
    here = pl.BlockSpec((TOK, BLK), lambda j: (0, j))
    return pl.pallas_call(
        feature_kernel,
        grid=(count,),
        in_specs=[pl.BlockSpec((TOK, BLK), cols(part)) for part in range(3)]
        + [pl.BlockSpec((SHORT - 1, BLK), cols(part)) for part in range(3)]
        + [pl.BlockSpec((1, PACK, LANES), taps(part)) for part in range(3)]
        + [
            pl.BlockSpec((TOK, BLK), cols(0)),
            pl.BlockSpec(shifts.shape, whole),
            pl.BlockSpec(sends.shape, whole),
        ],
        out_specs=[here, here, pl.BlockSpec((3, TOK, BLK), lambda j: (0, 0, j))],
        out_shape=[jax.ShapeDtypeStruct((TOK, wide), bf16)] * 2 + [pltpu.HBM((3, TOK, wide), f32)],
        compiler_params=pltpu.CompilerParams(vmem_limit_bytes=VMEM_LIMIT),
        cost_estimate=pl.CostEstimate(
            flops=2 * 3 * 768 * 144 * wide, bytes_accessed=12 * TOK * wide, transcendentals=0
        ),
        name="features",
    )(*[in_hbm(proj)] * 3, tail, tail, tail, params, params, params, in_hbm(grad_out), in_hbm(shifts), in_hbm(sends))


def main_kernel(
    gate_halo_ref, long_halo_ref, feat_ref, grad_ref, xq, xk, xv, tq, tk, tv, wq, wk, wv,
    skip_ref, filt_ref, mask_ref, unshift_ref, send_ref, *rest,
):
    (mixed_ref, source_ref, short_ref, lag_ref, skip_grad_ref, head_ref, end_ref,
     gate_ref, long_ref, long_out_ref, gate_grad_ref, feat_grad_ref, padded_ref,
     taps_ref, fore_ref, back_ref, ready_ref, sems) = rest[-18:]
    base = rest[0]
    count, step = pl.num_programs(0), pl.program_id(0)
    lane_group = lax.broadcasted_iota(jnp.int32, (TOK, LANES), 1) // GROUP

    def copies(at):
        slot = at % 2
        return [
            pltpu.make_async_copy(
                ready_ref.at[slot, part],
                source_ref.at[:, pl.ds(pl.multiple_of((part * BLOCKS + base + at) * BLK, BLK), BLK)],
                sems.at[slot, part],
            )
            for part in range(3)
        ]

    for part, (x, tail, taps) in enumerate(((xq, tq, wq), (xk, tk, wk), (xv, tv, wv))):
        padded_ref[part, :TOK] = x[...]
        padded_ref[part, TOK:] = tail_rows(tail)
        taps_ref[part] = tap_rows(taps)

    filt = filt_ref[0].astype(bf16)
    back_ref[...] = filt.astype(f32)
    fore_ref[...] = dot(filt, mask_ref[7])

    gate_ref[...] = (feat_ref[1] * feat_ref[2]).astype(bf16)
    long_ref[...] = (grad_ref[...].astype(f32) * feat_ref[0]).astype(bf16)

    def slab(at, carry):
        lanes = pl.ds(pl.multiple_of(at * LANES, LANES), LANES)
        own_long = long_ref[:, lanes]
        gates = jnp.concatenate([gate_ref[:, lanes], gate_halo_ref[:, lanes]], axis=0)
        longs = jnp.concatenate([own_long, long_halo_ref[:, lanes]], axis=0)
        turned = dot(mask_ref[6], own_long).astype(bf16)
        rows = pl.ds(pl.multiple_of(at * PER_SLAB, PER_SLAB), PER_SLAB)
        fore = fore_ref[rows, :]
        back = back_ref[rows, :]
        own_mask = mask_ref[4].astype(f32)
        before_mask = mask_ref[5].astype(f32)
        def bands(rows_of, first, second):
            made = []
            for g in range(PER_SLAB):
                band = jnp.broadcast_to(rows_of[g : g + 1], (TOK, LANES))
                band = pltpu.roll(band, 0, 1, stride=1, stride_axis=0).astype(bf16)
                made.append(jnp.concatenate([band * first, band * second], axis=1))
            return jnp.concatenate(made, axis=0)

        def gathered(wide):
            total = wide[:TOK]
            for g in range(1, PER_SLAB):
                total = jnp.where(lane_group == g, wide[g * TOK : (g + 1) * TOK], total)
            return total

        out = gathered(dot(bands(fore, mask_ref[0], mask_ref[1]), gates))
        spread = gathered(dot(bands(back, mask_ref[2], mask_ref[3]), longs))
        picked = jnp.concatenate(
            [jnp.where(lane_group == g, turned, jnp.zeros_like(turned)) for g in range(PER_SLAB)], axis=0
        )
        product = lax.dot_general(picked, gates, (((1,), (1,)), ((), ())), preferred_element_type=f32)
        sums = []
        for g in range(PER_SLAB):
            place = slice(g * TOK, (g + 1) * TOK)
            kept = product[place, :TOK] * own_mask + product[place, TOK:] * before_mask
            kept = pltpu.roll(kept, 0, 1, stride=1, stride_axis=0)
            sums.append(jnp.sum(kept, axis=0, keepdims=True))
        long_out_ref[:, lanes] = out
        gate_grad_ref[:, lanes] = spread
        lag_ref[rows, :] = jnp.concatenate(sums, axis=0)
        return carry

    lax.fori_loop(0, SLABS, slab, 0, unroll=UNROLL)
    gate = gate_ref[...].astype(f32)
    upstream = grad_ref[...].astype(f32)
    query = feat_ref[0]
    skip = tap_rows(skip_ref)[7:8]
    combined = long_out_ref[...] + skip * gate
    through = upstream * query
    mixed_ref[...] = (query * combined).astype(bf16)
    feat_grad_ref[0] = upstream * combined
    gate_grad = gate_grad_ref[...] + skip * through
    feat_grad_ref[1] = gate_grad * feat_ref[2]
    feat_grad_ref[2] = gate_grad * feat_ref[1]
    skip_grad = jnp.sum(through * gate, axis=0, keepdims=True)
    for k in range(SLABS):
        skip_grad_ref[k] = skip_grad[:, k * LANES : (k + 1) * LANES]

    @pl.when(step >= 2)
    def _():
        for copy in copies(step - 2):
            copy.wait()

    def column_part(part, carry):
        feat_grad = feat_grad_ref[part]
        moved = dot(unshift_ref[...], feat_grad.astype(bf16))
        near = padded_ref[part, :TOK].astype(f32)
        tail = padded_ref[part, TOK:].astype(f32)
        sums = [jnp.sum(near * feat_grad, axis=0, keepdims=True)]
        for lag in range(1, SHORT):
            first = (lag - 1) * WIDE
            own = jnp.sum(near * moved[first : first + TOK], axis=0, keepdims=True)
            before = jnp.sum(tail * moved[first + TOK : first + WIDE], axis=0, keepdims=True)
            sums.append(own + before)
        sums.append(jnp.zeros_like(sums[0]))
        sums = jnp.concatenate(sums, axis=0)
        for k in range(SLABS):
            short_ref[part, k] = sums[:, k * LANES : (k + 1) * LANES]
        source = short_sum(taps_ref[part], feat_grad, moved, WIDE)
        ready_ref[step % 2, part] = source.astype(bf16)
        end_ref[part] = source[TOK - 8 :]
        head_ref[part] = (feat_grad[:TAIL] * send_ref[:TAIL, 1:2]).astype(bf16)
        return carry

    lax.fori_loop(0, 3, column_part, 0)
    for copy in copies(step):
        copy.start()

    @pl.when(step == count - 1)
    def _():
        @pl.when(count >= 2)
        def _():
            for copy in copies(step - 1):
                copy.wait()

        for copy in copies(step):
            copy.wait()


def main_call(chunk, gate_halo, long_halo, feats, grad_out, proj, tail, params,
              masks, unshifts, sends, per_shard, kept):
    base, count = chunk
    shards = params.shape[0]
    own_blocks = BLOCKS // shards
    local = pl.BlockSpec((TOK, BLK), lambda j: (0, j))
    first_cols = pl.BlockSpec((TOK, BLK), lambda j: (0, base + j))

    def cols(rows, part):
        return pl.BlockSpec((rows, BLK), lambda j: (0, part * BLOCKS + base + j))

    def taps(part):
        def index(j):
            place = part * BLOCKS + base + j
            return (place // per_shard, place % per_shard, 0)

        return pl.BlockSpec((1, PACK, LANES), index)

    def skips(j):
        return ((base + j) // own_blocks, (base + j) % own_blocks, 0)

    def filters(j):
        return ((base + j) // own_blocks, per_shard + (base + j) % own_blocks, 0)

    def whole(array):
        return pl.BlockSpec(array.shape, lambda j: (0,) * array.ndim)

    groups = BLK // GROUP
    operands = [gate_halo, long_halo, feats, in_hbm(grad_out), *[in_hbm(proj)] * 3, tail, tail, tail,
                params, params, params, params, params, *[in_hbm(table) for table in (masks, unshifts, sends)]]
    in_specs = (
        [local, local, pl.BlockSpec((3, TOK, BLK), lambda j: (0, 0, j)), first_cols]
        + [cols(TOK, part) for part in range(3)]
        + [cols(SHORT - 1, part) for part in range(3)]
        + [taps(part) for part in range(3)]
        + [pl.BlockSpec((1, PACK, LANES), skips), pl.BlockSpec((1, PACK, LANES), filters)]
        + [whole(masks), whole(unshifts), whole(sends)]
    )
    aliases = {}
    if kept is not None:
        aliases = {len(operands) + k: k for k in range(len(kept))}
        operands = operands + list(kept)
        in_specs = in_specs + [pl.BlockSpec(memory_space=pl.ANY)] * len(kept)
    slabs = C // LANES
    places = len(operands) - (0 if kept is None else len(kept))

    def kernel(*refs):
        main_kernel(*refs[:places], base, *refs[places:])

    return pl.pallas_call(
        kernel,
        grid=(count,),
        in_specs=in_specs,
        out_specs=[
            first_cols,
            pl.BlockSpec(memory_space=pl.ANY),
            pl.BlockSpec((3, SLABS, 8, LANES), lambda j: (0, base + j, 0, 0)),
            pl.BlockSpec((groups, LANES), lambda j: (base + j, 0)),
            pl.BlockSpec((SLABS, 1, LANES), lambda j: (base + j, 0, 0)),
            pl.BlockSpec((3, TAIL, BLK), lambda j: (0, 0, base + j)),
            pl.BlockSpec((3, 8, BLK), lambda j: (0, 0, base + j)),
        ],
        out_shape=[
            jax.ShapeDtypeStruct((TOK, C), bf16),
            jax.ShapeDtypeStruct((TOK, 3 * C), bf16),
            jax.ShapeDtypeStruct((3, slabs, 8, LANES), f32),
            jax.ShapeDtypeStruct((C // GROUP, LANES), f32),
            jax.ShapeDtypeStruct((slabs, 1, LANES), f32),
            jax.ShapeDtypeStruct((3, TAIL, C), bf16),
            jax.ShapeDtypeStruct((3, 8, C), f32),
        ],
        scratch_shapes=[
            pltpu.VMEM((TOK, BLK), bf16),
            pltpu.VMEM((TOK, BLK), bf16),
            pltpu.VMEM((TOK, BLK), f32),
            pltpu.VMEM((TOK, BLK), f32),
            pltpu.VMEM((3, TOK, BLK), f32),
            pltpu.VMEM((3, TOK + TAIL, BLK), bf16),
            pltpu.VMEM((3, 8, BLK), f32),
            pltpu.VMEM((PACK, LANES), f32),
            pltpu.VMEM((PACK, LANES), f32),
            pltpu.VMEM((2, 3, TOK, BLK), bf16),
            pltpu.SemaphoreType.DMA((2, 3)),
        ],
        input_output_aliases=aliases,
        compiler_params=pltpu.CompilerParams(vmem_limit_bytes=VMEM_LIMIT),
        cost_estimate=pl.CostEstimate(
            flops=5_000_000_000 * count, bytes_accessed=40 * TOK * count * BLK, transcendentals=0
        ),
        name="main",
    )(*operands)


def patch_kernel(starts_ref, source_ref, end_ref, head_ref, params_ref, out_ref):
    rows = lax.broadcasted_iota(jnp.int32, (8, BLK), 0) + (TOK - 8)
    listed = starts_ref[...]
    last = jnp.max(jnp.where(listed < TOK, listed, -FAR), axis=1, keepdims=True)
    keep = jnp.where(rows >= last, 1.0, 0.0)
    shards = params_ref.shape[0]
    per_shard = 3 * BLOCKS // shards
    for place in range(3 * BLOCKS):
        part, first = place // BLOCKS, place % BLOCKS * BLK
        own = slice(first, first + BLK)
        empty = jnp.zeros((8, BLK), f32)
        ahead = jnp.concatenate([empty, head_ref[part, :, own].astype(f32), empty[: 9 - SHORT]], axis=0)
        first = place % per_shard * PACK
        taps = tap_rows(params_ref[pl.ds(place // per_shard, 1), first : first + PACK])
        extra = empty
        for lag in range(1, SHORT):
            extra = extra + taps[lag : lag + 1] * ahead[lag : lag + 8]
        final = end_ref[part, :, own] + extra * keep
        lanes = slice(place * BLK, (place + 1) * BLK)
        before = source_ref[:, lanes].astype(f32)[:8]
        out_ref[:, lanes] = jnp.concatenate([before, final], axis=0).astype(bf16)


def patch_call(starts, source, end, head, params):
    rows = TOK // TAIL - 1

    def whole(array):
        return pl.BlockSpec(array.shape, lambda j: (0,) * array.ndim)

    strip = pl.BlockSpec((TAIL, 3 * C), lambda j: (rows, 0))
    return pl.pallas_call(
        patch_kernel,
        grid=(1,),
        in_specs=[whole(starts), strip, whole(end), whole(head), whole(params)],
        out_specs=strip,
        out_shape=jax.ShapeDtypeStruct(source.shape, bf16),
        input_output_aliases={1: 0},
        compiler_params=pltpu.CompilerParams(vmem_limit_bytes=VMEM_LIMIT),
        cost_estimate=pl.CostEstimate(flops=1_000_000, bytes_accessed=2_000_000, transcendentals=0),
        name="patch",
    )(starts, source, end, head, params)


def prepare_kernel(starts_hbm, source_hbm, taps_hbm, skip_hbm, filt_hbm, tail_ref, packed_ref,
                   starts_ref, source_ref, taps_ref, skip_ref, filt_ref, sems):
    copies = [
        pltpu.make_async_copy(starts_hbm, starts_ref, sems.at[0]),
        pltpu.make_async_copy(source_hbm.at[pl.ds(TOK - TAIL, TAIL), :], source_ref, sems.at[1]),
        pltpu.make_async_copy(taps_hbm, taps_ref, sems.at[2]),
        pltpu.make_async_copy(skip_hbm, skip_ref, sems.at[3]),
        pltpu.make_async_copy(filt_hbm, filt_ref, sems.at[4]),
    ]
    for copy in copies:
        copy.start()
    for copy in copies:
        copy.wait()
    listed = starts_ref[...]
    last = jnp.max(jnp.where(listed < TOK, listed, -FAR), axis=1, keepdims=True)
    rows = lax.broadcasted_iota(jnp.int32, (SHORT - 1, 1), 0) + (TOK - SHORT + 1)
    tail = source_ref[...].astype(f32)[TAIL - SHORT + 1 :]
    tail_ref[...] = (tail * jnp.where(rows >= last, 1.0, 0.0)).astype(bf16)
    own, slabs = skip_ref.shape[1], taps_ref.shape[1] // LANES
    empty = jnp.zeros((1, LANES), f32)
    rows = []
    for k in range(slabs):
        lanes = slice(k * LANES, (k + 1) * LANES)
        rows += [taps_ref[:, lanes], skip_ref[:, lanes] if k * LANES < own else empty]
    packed = jnp.concatenate(rows + [filt_ref[...]], axis=0)
    packed_ref[...] = packed


def prepare_call(starts, source, short_taps, skip, filt, shards):
    own = skip.shape[0]
    rows = short_taps.shape[1] // LANES * 8 + filt.shape[0]
    return pl.pallas_call(
        prepare_kernel,
        in_specs=[pl.BlockSpec(memory_space=pltpu.HBM)] * 5,
        out_specs=[pl.BlockSpec(memory_space=pltpu.VMEM)] * 2,
        out_shape=[
            jax.ShapeDtypeStruct((SHORT - 1, 3 * C), bf16),
            jax.ShapeDtypeStruct((rows, LANES), f32),
        ],
        scratch_shapes=[
            pltpu.VMEM(starts.shape, jnp.int32),
            pltpu.VMEM((TAIL, 3 * C), bf16),
            pltpu.VMEM(short_taps.shape, f32),
            pltpu.VMEM((1, own), f32),
            pltpu.VMEM(filt.shape, f32),
            pltpu.SemaphoreType.DMA((5,)),
        ],
        compiler_params=pltpu.CompilerParams(vmem_limit_bytes=VMEM_LIMIT),
        cost_estimate=pl.CostEstimate(flops=1_000_000, bytes_accessed=2_000_000, transcendentals=0),
        name="prepare",
    )(*[in_hbm(array) for array in (starts, source, short_taps, skip[None], filt)])


def body(proj, short_taps, long_filter, skip, grad_out, starts):
    shards, count = lax.axis_size("fsdp"), lax.axis_size("ctx")
    source, upstream = proj[0], grad_out[0]
    shifts, sends = shift_call(starts[0])
    masks, unshifts = link_call(starts[0])
    wide = short_taps.shape[1]
    per_shard = wide // BLK
    tail, packed = prepare_call(starts[0], source, short_taps, skip, long_filter.T, shards)
    tail = ring(tail, 1)
    params = lax.all_gather(packed, "fsdp", axis=0)
    parts = []
    for chunk in CHUNKS:
        gate_send, long_send, feats = feature_call(
            chunk, source, tail, params, upstream, shifts, sends, per_shard
        )
        parts.append((ring(gate_send, 1), ring(long_send, -1), feats))
    kept = None
    for chunk, part in zip(CHUNKS, parts):
        kept = main_call(
            chunk, *part, upstream, source, tail, params, masks, unshifts,
            sends, per_shard, kept,
        )
    mixed, grad_source, short_sums, lag_sums, skip_sums, head, end = kept
    head = ring(head[:, : SHORT - 1], -1)

    skip_slabs = C // LANES // shards
    skip_sums = skip_sums.reshape(shards, skip_slabs, 1, LANES)
    short_sums = short_sums.reshape(shards, -1, 8, LANES)
    room = ((0, 0), (0, short_sums.shape[1] - skip_slabs), (7, 0), (0, 0))
    short_sums = short_sums + jnp.pad(skip_sums, room)
    sums = jnp.concatenate(
        [short_sums.reshape(shards, -1, LANES), lag_sums.reshape(shards, -1, LANES)], axis=1
    )
    piece = sums.shape[1] // count
    sums = sums.reshape(shards * count, piece, LANES)
    sums = lax.all_to_all(sums.astype(bf16), ("fsdp", "ctx"), 0, 0, tiled=True)
    sums = jnp.sum(sums.astype(f32), axis=0)
    sums = sums * (float(shards * count * TOK) ** -0.5)
    grad_source = patch_call(starts[0], grad_source, end, head, params)
    sums = lax.all_to_all(
        jnp.broadcast_to(sums[None], (count,) + sums.shape), "ctx", 0, 0, tiled=True
    ).reshape(count * piece, LANES)
    slabs = 3 * C // LANES // shards
    grad_short = sums[: slabs * 8].reshape(slabs, 8, LANES)
    grad_skip = grad_short[:skip_slabs, 7].reshape(-1)
    grad_short = grad_short[:, :SHORT].transpose(1, 0, 2).reshape(SHORT, -1)
    grad_long = sums[slabs * 8 :, ::-1].T
    return mixed[None], grad_source[None], grad_short, grad_long, grad_skip


def solution(mesh):
    placed = (
        P("fsdp", "ctx", None),
        P(None, "fsdp"),
        P(None, "fsdp"),
        P("fsdp"),
        P("fsdp", "ctx", None),
        P("fsdp", "ctx", None),
    )
    return jax.shard_map(
        body,
        mesh=mesh,
        in_specs=placed,
        out_specs=(
            P("fsdp", "ctx", None),
            P("fsdp", "ctx", None),
            P(None, "fsdp"),
            P(None, "fsdp"),
            P("fsdp"),
        ),
        check_vma=False,
    )
```

```python
import functools

import jax
import jax.numpy as jnp
from jax import lax
from jax.experimental import pallas as pl
from jax.experimental.pallas import tpu as pltpu
from jax.sharding import PartitionSpec as P

C = 4096
GROUP = 16
LEN = 128
SHORT = 7
TOK = 128
TAIL = 16
WIDE = TOK + TAIL
LANES = 128
BLK = 512
SLABS = BLK // LANES
PER_SLAB = LANES // GROUP
BLOCKS = C // BLK
UNROLL = 4
CHUNKS = ((0, 2), (2, 2), (4, 2), (6, 2))
PACK = 32
FAR = 1 << 20
VMEM_LIMIT = 48 * 1024 * 1024

bf16 = jnp.bfloat16
f32 = jnp.float32


def ring(block, distance):
    count = lax.axis_size("ctx")
    return lax.ppermute(block, "ctx", [(i, (i + distance) % count) for i in range(count)])


def dot(a, b):
    return jnp.dot(a, b, preferred_element_type=f32)


def in_hbm(array):
    return pltpu.with_memory_space_constraint(array, pltpu.HBM)


def latest_start(listed, places):
    latest = jnp.full(places.shape, -FAR, jnp.int32)
    for k in range(listed.shape[1]):
        start = listed[:, k : k + 1]
        latest = jnp.maximum(latest, jnp.where((start < TOK) & (start <= places), start, -FAR))
    return latest


def put(ref, place, linked):
    ref[place] = jnp.where(linked, 1.0, 0.0).astype(ref.dtype)


def bounds(listed):
    usable = listed < TOK
    first = jnp.min(jnp.where(usable, listed, FAR), axis=1, keepdims=True)
    last = jnp.max(jnp.where(usable, listed, -FAR), axis=1, keepdims=True)
    return first, last


def shift_kernel(starts_ref, shift_ref, send_ref):
    listed = starts_ref[...]
    first, last = bounds(listed)
    here = lax.broadcasted_iota(jnp.int32, (TOK, WIDE), 0)
    cols = lax.broadcasted_iota(jnp.int32, (TOK, WIDE), 1)
    cols = jnp.where(cols < TOK, cols, jnp.where(cols < TOK + SHORT - 1, cols - (TOK + SHORT - 1), FAR))
    latest_here = latest_start(listed, here)
    for lag in range(1, SHORT):
        place = slice((lag - 1) * TOK, lag * TOK)
        put(shift_ref, place, (cols == here - lag) & (latest_here <= here - lag))
    side = lax.broadcasted_iota(jnp.int32, (TOK, 2), 1)
    rows = lax.broadcasted_iota(jnp.int32, (TOK, 2), 0)
    put(send_ref, slice(0, TOK), jnp.where(side == 0, rows - last, first - 1 - rows) >= 0)


def link_kernel(starts_ref, mask_ref, unshift_ref):
    listed = starts_ref[...]
    first, last = bounds(listed)
    t = lax.broadcasted_iota(jnp.int32, (TOK, TOK), 0)
    s = lax.broadcasted_iota(jnp.int32, (TOK, TOK), 1)
    back = TOK - 1 - t
    latest_t, latest_s = latest_start(listed, t), latest_start(listed, s)
    put(mask_ref, 0, (s <= t) & (latest_t <= s))
    put(mask_ref, 1, (s > t) & (t < first))
    put(mask_ref, 2, (t <= s) & (latest_s <= t))
    put(mask_ref, 3, (t > s) & (t >= last))
    put(mask_ref, 4, (s <= back) & (latest_start(listed, back) <= s))
    put(mask_ref, 5, (s > back) & (back < first))
    put(mask_ref, 6, s == back)
    put(mask_ref, 7, (s + t == TOK) | (s + t == 0))
    rows = lax.broadcasted_iota(jnp.int32, (TAIL, TOK), 0)
    tail = jnp.where(rows < SHORT - 1, rows - (SHORT - 1), FAR)
    later = lax.broadcasted_iota(jnp.int32, (TAIL, TOK), 1)
    latest_later = latest_start(listed, later)
    for lag in range(1, SHORT):
        first_row = (lag - 1) * WIDE
        put(unshift_ref, slice(first_row, first_row + TOK), (s == t + lag) & (latest_s <= t))
        linked = (later == tail + lag) & (latest_later <= tail)
        put(unshift_ref, slice(first_row + TOK, first_row + WIDE), linked)


def table_call(kernel, shapes, starts, name):
    return pl.pallas_call(
        kernel,
        in_specs=[pl.BlockSpec(memory_space=pltpu.VMEM)],
        out_specs=[pl.BlockSpec(memory_space=pltpu.VMEM)] * 2,
        out_shape=[jax.ShapeDtypeStruct(shape, dtype) for shape, dtype in shapes],
        cost_estimate=pl.CostEstimate(flops=5_000_000, bytes_accessed=1_000_000, transcendentals=0),
        name=name,
    )(starts)


def shift_call(starts):
    shapes = [(((SHORT - 1) * TOK, WIDE), bf16), ((TOK, 2), f32)]
    return table_call(shift_kernel, shapes, starts, "shifts")


def link_call(starts):
    shapes = [((8, TOK, TOK), bf16), (((SHORT - 1) * WIDE, TOK), bf16)]
    return table_call(link_kernel, shapes, starts, "links")


def short_sum(taps, near, moved, step):
    total = taps[0:1] * near
    for lag in range(1, SHORT):
        first = (lag - 1) * step
        total = total + taps[lag : lag + 1] * moved[first : first + TOK]
    return total


def tap_rows(packed):
    return jnp.concatenate([packed[0, 8 * k : 8 * k + 8] for k in range(SLABS)], axis=1)


def tail_rows(tail):
    tail = tail[...].astype(f32)
    empty = jnp.zeros((TAIL - tail.shape[0], tail.shape[1]), f32)
    return jnp.concatenate([tail, empty], axis=0).astype(bf16)


def feature_kernel(
    xq, xk, xv, tq, tk, tv, wq, wk, wv, grad_ref, shift_ref, send_ref,
    gate_send_ref, long_send_ref, feat_ref,
):
    feats = []
    for part, (x, tail, taps) in enumerate(((xq, tq, wq), (xk, tk, wk), (xv, tv, wv))):
        own = x[...]
        moved = dot(shift_ref[...], jnp.concatenate([own, tail_rows(tail)], axis=0))
        feats.append(short_sum(tap_rows(taps), own.astype(f32), moved, TOK))
        feat_ref[part] = feats[part]
    gate = (feats[1] * feats[2]).astype(bf16)
    long_in = (grad_ref[...].astype(f32) * feats[0]).astype(bf16)
    gate_send_ref[...] = (gate.astype(f32) * send_ref[:, 0:1]).astype(bf16)
    long_send_ref[...] = (long_in.astype(f32) * send_ref[:, 1:2]).astype(bf16)


def feature_call(chunk, proj, tail, params, grad_out, shifts, sends, per_shard):
    base, count = chunk
    wide = count * BLK

    def cols(part):
        return lambda j: (0, part * BLOCKS + base + j)

    def taps(part):
        def index(j):
            place = part * BLOCKS + base + j
            return (place // per_shard, place % per_shard, 0)

        return index

    whole = lambda j: (0, 0)
    here = pl.BlockSpec((TOK, BLK), lambda j: (0, j))
    return pl.pallas_call(
        feature_kernel,
        grid=(count,),
        in_specs=[pl.BlockSpec((TOK, BLK), cols(part)) for part in range(3)]
        + [pl.BlockSpec((SHORT - 1, BLK), cols(part)) for part in range(3)]
        + [pl.BlockSpec((1, PACK, LANES), taps(part)) for part in range(3)]
        + [
            pl.BlockSpec((TOK, BLK), cols(0)),
            pl.BlockSpec(shifts.shape, whole),
            pl.BlockSpec(sends.shape, whole),
        ],
        out_specs=[here, here, pl.BlockSpec((3, TOK, BLK), lambda j: (0, 0, j))],
        out_shape=[jax.ShapeDtypeStruct((TOK, wide), bf16)] * 2 + [pltpu.HBM((3, TOK, wide), f32)],
        compiler_params=pltpu.CompilerParams(vmem_limit_bytes=VMEM_LIMIT),
        cost_estimate=pl.CostEstimate(
            flops=2 * 3 * 768 * 144 * wide, bytes_accessed=12 * TOK * wide, transcendentals=0
        ),
        name="features",
    )(*[in_hbm(proj)] * 3, tail, tail, tail, params, params, params, in_hbm(grad_out), in_hbm(shifts), in_hbm(sends))


def main_kernel(
    gate_halo_ref, long_halo_ref, feat_ref, grad_ref, xq, xk, xv, tq, tk, tv, wq, wk, wv,
    skip_ref, filt_ref, mask_ref, unshift_ref, send_ref, *rest,
):
    (mixed_ref, source_ref, short_ref, lag_ref, skip_grad_ref, head_ref, end_ref,
     gate_ref, long_ref, long_out_ref, gate_grad_ref, feat_grad_ref, padded_ref,
     taps_ref, fore_ref, back_ref, ready_ref, sems) = rest[-18:]
    base = rest[0]
    count, step = pl.num_programs(0), pl.program_id(0)
    lane_group = lax.broadcasted_iota(jnp.int32, (TOK, LANES), 1) // GROUP

    def copies(at):
        slot = at % 2
        return [
            pltpu.make_async_copy(
                ready_ref.at[slot, part],
                source_ref.at[:, pl.ds(pl.multiple_of((part * BLOCKS + base + at) * BLK, BLK), BLK)],
                sems.at[slot, part],
            )
            for part in range(3)
        ]

    for part, (x, tail, taps) in enumerate(((xq, tq, wq), (xk, tk, wk), (xv, tv, wv))):
        padded_ref[part, :TOK] = x[...]
        padded_ref[part, TOK:] = tail_rows(tail)
        taps_ref[part] = tap_rows(taps)

    filt = filt_ref[0].astype(bf16)
    back_ref[...] = filt.astype(f32)
    fore_ref[...] = dot(filt, mask_ref[7])

    gate_ref[...] = (feat_ref[1] * feat_ref[2]).astype(bf16)
    long_ref[...] = (grad_ref[...].astype(f32) * feat_ref[0]).astype(bf16)

    def slab(at, carry):
        lanes = pl.ds(pl.multiple_of(at * LANES, LANES), LANES)
        own_long = long_ref[:, lanes]
        gates = jnp.concatenate([gate_ref[:, lanes], gate_halo_ref[:, lanes]], axis=0)
        longs = jnp.concatenate([own_long, long_halo_ref[:, lanes]], axis=0)
        turned = dot(mask_ref[6], own_long).astype(bf16)
        rows = pl.ds(pl.multiple_of(at * PER_SLAB, PER_SLAB), PER_SLAB)
        fore = fore_ref[rows, :]
        back = back_ref[rows, :]
        own_mask = mask_ref[4].astype(f32)
        before_mask = mask_ref[5].astype(f32)
        def bands(rows_of, first, second):
            made = []
            for g in range(PER_SLAB):
                band = jnp.broadcast_to(rows_of[g : g + 1], (TOK, LANES))
                band = pltpu.roll(band, 0, 1, stride=1, stride_axis=0).astype(bf16)
                made.append(jnp.concatenate([band * first, band * second], axis=1))
            return jnp.concatenate(made, axis=0)

        def gathered(wide):
            total = wide[:TOK]
            for g in range(1, PER_SLAB):
                total = jnp.where(lane_group == g, wide[g * TOK : (g + 1) * TOK], total)
            return total

        out = gathered(dot(bands(fore, mask_ref[0], mask_ref[1]), gates))
        spread = gathered(dot(bands(back, mask_ref[2], mask_ref[3]), longs))
        picked = jnp.concatenate(
            [jnp.where(lane_group == g, turned, jnp.zeros_like(turned)) for g in range(PER_SLAB)], axis=0
        )
        product = lax.dot_general(picked, gates, (((1,), (1,)), ((), ())), preferred_element_type=f32)
        sums = []
        for g in range(PER_SLAB):
            place = slice(g * TOK, (g + 1) * TOK)
            kept = product[place, :TOK] * own_mask + product[place, TOK:] * before_mask
            kept = pltpu.roll(kept, 0, 1, stride=1, stride_axis=0)
            sums.append(jnp.sum(kept, axis=0, keepdims=True))
        long_out_ref[:, lanes] = out
        gate_grad_ref[:, lanes] = spread
        lag_ref[rows, :] = dot(jnp.concatenate(sums, axis=0).astype(bf16), mask_ref[6])
        return carry

    lax.fori_loop(0, SLABS, slab, 0, unroll=UNROLL)
    gate = gate_ref[...].astype(f32)
    upstream = grad_ref[...].astype(f32)
    query = feat_ref[0]
    skip = tap_rows(skip_ref)[7:8]
    combined = long_out_ref[...] + skip * gate
    through = upstream * query
    mixed_ref[...] = (query * combined).astype(bf16)
    feat_grad_ref[0] = upstream * combined
    gate_grad = gate_grad_ref[...] + skip * through
    feat_grad_ref[1] = gate_grad * feat_ref[2]
    feat_grad_ref[2] = gate_grad * feat_ref[1]
    skip_grad = jnp.sum(through * gate, axis=0, keepdims=True)
    for k in range(SLABS):
        skip_grad_ref[k] = skip_grad[:, k * LANES : (k + 1) * LANES]

    @pl.when(step >= 2)
    def _():
        for copy in copies(step - 2):
            copy.wait()

    def column_part(part, carry):
        feat_grad = feat_grad_ref[part]
        moved = dot(unshift_ref[...], feat_grad.astype(bf16))
        near = padded_ref[part, :TOK].astype(f32)
        tail = padded_ref[part, TOK:].astype(f32)
        sums = [jnp.sum(near * feat_grad, axis=0, keepdims=True)]
        for lag in range(1, SHORT):
            first = (lag - 1) * WIDE
            own = jnp.sum(near * moved[first : first + TOK], axis=0, keepdims=True)
            before = jnp.sum(tail * moved[first + TOK : first + WIDE], axis=0, keepdims=True)
            sums.append(own + before)
        sums.append(jnp.zeros_like(sums[0]))
        sums = jnp.concatenate(sums, axis=0)
        for k in range(SLABS):
            short_ref[part, k] = sums[:, k * LANES : (k + 1) * LANES]
        source = short_sum(taps_ref[part], feat_grad, moved, WIDE)
        ready_ref[step % 2, part] = source.astype(bf16)
        end_ref[part] = source[TOK - 8 :]
        head_ref[part] = (feat_grad[:TAIL] * send_ref[:TAIL, 1:2]).astype(bf16)
        return carry

    lax.fori_loop(0, 3, column_part, 0)
    for copy in copies(step):
        copy.start()

    @pl.when(step == count - 1)
    def _():
        @pl.when(count >= 2)
        def _():
            for copy in copies(step - 1):
                copy.wait()

        for copy in copies(step):
            copy.wait()


def main_call(chunk, gate_halo, long_halo, feats, grad_out, proj, tail, params,
              masks, unshifts, sends, per_shard, kept):
    base, count = chunk
    shards = params.shape[0]
    own_blocks = BLOCKS // shards
    local = pl.BlockSpec((TOK, BLK), lambda j: (0, j))
    first_cols = pl.BlockSpec((TOK, BLK), lambda j: (0, base + j))

    def cols(rows, part):
        return pl.BlockSpec((rows, BLK), lambda j: (0, part * BLOCKS + base + j))

    def taps(part):
        def index(j):
            place = part * BLOCKS + base + j
            return (place // per_shard, place % per_shard, 0)

        return pl.BlockSpec((1, PACK, LANES), index)

    def skips(j):
        return ((base + j) // own_blocks, (base + j) % own_blocks, 0)

    def filters(j):
        return ((base + j) // own_blocks, per_shard + (base + j) % own_blocks, 0)

    def whole(array):
        return pl.BlockSpec(array.shape, lambda j: (0,) * array.ndim)

    groups = BLK // GROUP
    operands = [gate_halo, long_halo, feats, in_hbm(grad_out), *[in_hbm(proj)] * 3, tail, tail, tail,
                params, params, params, params, params, masks, unshifts, sends]
    in_specs = (
        [local, local, pl.BlockSpec((3, TOK, BLK), lambda j: (0, 0, j)), first_cols]
        + [cols(TOK, part) for part in range(3)]
        + [cols(SHORT - 1, part) for part in range(3)]
        + [taps(part) for part in range(3)]
        + [pl.BlockSpec((1, PACK, LANES), skips), pl.BlockSpec((1, PACK, LANES), filters)]
        + [whole(masks), whole(unshifts), whole(sends)]
    )
    aliases = {}
    if kept is not None:
        aliases = {len(operands) + k: k for k in range(len(kept))}
        operands = operands + list(kept)
        in_specs = in_specs + [pl.BlockSpec(memory_space=pl.ANY)] * len(kept)
    slabs = C // LANES
    places = len(operands) - (0 if kept is None else len(kept))

    def kernel(*refs):
        main_kernel(*refs[:places], base, *refs[places:])

    return pl.pallas_call(
        kernel,
        grid=(count,),
        in_specs=in_specs,
        out_specs=[
            first_cols,
            pl.BlockSpec(memory_space=pl.ANY),
            pl.BlockSpec((3, SLABS, 8, LANES), lambda j: (0, base + j, 0, 0)),
            pl.BlockSpec((groups, LANES), lambda j: (base + j, 0)),
            pl.BlockSpec((SLABS, 1, LANES), lambda j: (base + j, 0, 0)),
            pl.BlockSpec((3, TAIL, BLK), lambda j: (0, 0, base + j)),
            pl.BlockSpec((3, 8, BLK), lambda j: (0, 0, base + j)),
        ],
        out_shape=[
            jax.ShapeDtypeStruct((TOK, C), bf16),
            jax.ShapeDtypeStruct((TOK, 3 * C), bf16),
            jax.ShapeDtypeStruct((3, slabs, 8, LANES), f32),
            jax.ShapeDtypeStruct((C // GROUP, LANES), f32),
            jax.ShapeDtypeStruct((slabs, 1, LANES), f32),
            jax.ShapeDtypeStruct((3, TAIL, C), bf16),
            jax.ShapeDtypeStruct((3, 8, C), f32),
        ],
        scratch_shapes=[
            pltpu.VMEM((TOK, BLK), bf16),
            pltpu.VMEM((TOK, BLK), bf16),
            pltpu.VMEM((TOK, BLK), f32),
            pltpu.VMEM((TOK, BLK), f32),
            pltpu.VMEM((3, TOK, BLK), f32),
            pltpu.VMEM((3, TOK + TAIL, BLK), bf16),
            pltpu.VMEM((3, 8, BLK), f32),
            pltpu.VMEM((PACK, LANES), f32),
            pltpu.VMEM((PACK, LANES), f32),
            pltpu.VMEM((2, 3, TOK, BLK), bf16),
            pltpu.SemaphoreType.DMA((2, 3)),
        ],
        input_output_aliases=aliases,
        compiler_params=pltpu.CompilerParams(vmem_limit_bytes=VMEM_LIMIT),
        cost_estimate=pl.CostEstimate(
            flops=5_000_000_000 * count, bytes_accessed=40 * TOK * count * BLK, transcendentals=0
        ),
        name="main",
    )(*operands)


def patch_kernel(starts_ref, source_ref, end_ref, head_ref, params_ref, out_ref):
    rows = lax.broadcasted_iota(jnp.int32, (8, BLK), 0) + (TOK - 8)
    listed = starts_ref[...]
    last = jnp.max(jnp.where(listed < TOK, listed, -FAR), axis=1, keepdims=True)
    keep = jnp.where(rows >= last, 1.0, 0.0)
    shards = params_ref.shape[0]
    per_shard = 3 * BLOCKS // shards
    for place in range(3 * BLOCKS):
        part, first = place // BLOCKS, place % BLOCKS * BLK
        own = slice(first, first + BLK)
        empty = jnp.zeros((8, BLK), f32)
        ahead = jnp.concatenate([empty, head_ref[part, :, own].astype(f32), empty[: 9 - SHORT]], axis=0)
        first = place % per_shard * PACK
        taps = tap_rows(params_ref[pl.ds(place // per_shard, 1), first : first + PACK])
        extra = empty
        for lag in range(1, SHORT):
            extra = extra + taps[lag : lag + 1] * ahead[lag : lag + 8]
        final = end_ref[part, :, own] + extra * keep
        lanes = slice(place * BLK, (place + 1) * BLK)
        before = source_ref[:, lanes].astype(f32)[:8]
        out_ref[:, lanes] = jnp.concatenate([before, final], axis=0).astype(bf16)


def patch_call(starts, source, end, head, params):
    rows = TOK // TAIL - 1

    def whole(array):
        return pl.BlockSpec(array.shape, lambda j: (0,) * array.ndim)

    strip = pl.BlockSpec((TAIL, 3 * C), lambda j: (rows, 0))
    return pl.pallas_call(
        patch_kernel,
        grid=(1,),
        in_specs=[whole(starts), strip, whole(end), whole(head), whole(params)],
        out_specs=strip,
        out_shape=jax.ShapeDtypeStruct(source.shape, bf16),
        input_output_aliases={1: 0},
        compiler_params=pltpu.CompilerParams(vmem_limit_bytes=VMEM_LIMIT),
        cost_estimate=pl.CostEstimate(flops=1_000_000, bytes_accessed=2_000_000, transcendentals=0),
        name="patch",
    )(starts, source, end, head, params)


def prepare_kernel(starts_hbm, source_hbm, taps_hbm, skip_hbm, filt_hbm, tail_ref, packed_ref,
                   starts_ref, source_ref, taps_ref, skip_ref, filt_ref, sems):
    copies = [
        pltpu.make_async_copy(starts_hbm, starts_ref, sems.at[0]),
        pltpu.make_async_copy(source_hbm.at[pl.ds(TOK - TAIL, TAIL), :], source_ref, sems.at[1]),
        pltpu.make_async_copy(taps_hbm, taps_ref, sems.at[2]),
        pltpu.make_async_copy(skip_hbm, skip_ref, sems.at[3]),
        pltpu.make_async_copy(filt_hbm, filt_ref, sems.at[4]),
    ]
    for copy in copies:
        copy.start()
    for copy in copies:
        copy.wait()
    listed = starts_ref[...]
    last = jnp.max(jnp.where(listed < TOK, listed, -FAR), axis=1, keepdims=True)
    rows = lax.broadcasted_iota(jnp.int32, (SHORT - 1, 1), 0) + (TOK - SHORT + 1)
    tail = source_ref[...].astype(f32)[TAIL - SHORT + 1 :]
    tail_ref[...] = (tail * jnp.where(rows >= last, 1.0, 0.0)).astype(bf16)
    own, slabs = skip_ref.shape[1], taps_ref.shape[1] // LANES
    empty = jnp.zeros((1, LANES), f32)
    rows = []
    for k in range(slabs):
        lanes = slice(k * LANES, (k + 1) * LANES)
        rows += [taps_ref[:, lanes], skip_ref[:, lanes] if k * LANES < own else empty]
    packed = jnp.concatenate(rows + [filt_ref[...]], axis=0)
    packed_ref[...] = packed


def prepare_call(starts, source, short_taps, skip, filt, shards):
    own = skip.shape[0]
    rows = short_taps.shape[1] // LANES * 8 + filt.shape[0]
    return pl.pallas_call(
        prepare_kernel,
        in_specs=[pl.BlockSpec(memory_space=pltpu.HBM)] * 5,
        out_specs=[pl.BlockSpec(memory_space=pltpu.VMEM)] * 2,
        out_shape=[
            jax.ShapeDtypeStruct((SHORT - 1, 3 * C), bf16),
            jax.ShapeDtypeStruct((rows, LANES), f32),
        ],
        scratch_shapes=[
            pltpu.VMEM(starts.shape, jnp.int32),
            pltpu.VMEM((TAIL, 3 * C), bf16),
            pltpu.VMEM(short_taps.shape, f32),
            pltpu.VMEM((1, own), f32),
            pltpu.VMEM(filt.shape, f32),
            pltpu.SemaphoreType.DMA((5,)),
        ],
        compiler_params=pltpu.CompilerParams(vmem_limit_bytes=VMEM_LIMIT),
        cost_estimate=pl.CostEstimate(flops=1_000_000, bytes_accessed=2_000_000, transcendentals=0),
        name="prepare",
    )(*[in_hbm(array) for array in (starts, source, short_taps, skip[None], filt)])


def body(proj, short_taps, long_filter, skip, grad_out, starts):
    shards, count = lax.axis_size("fsdp"), lax.axis_size("ctx")
    source, upstream = proj[0], grad_out[0]
    shifts, sends = shift_call(starts[0])
    masks, unshifts = link_call(starts[0])
    wide = short_taps.shape[1]
    per_shard = wide // BLK
    tail, packed = prepare_call(starts[0], source, short_taps, skip, long_filter.T, shards)
    tail = ring(tail, 1)
    params = lax.all_gather(packed, "fsdp", axis=0)
    parts = []
    for chunk in CHUNKS:
        gate_send, long_send, feats = feature_call(
            chunk, source, tail, params, upstream, shifts, sends, per_shard
        )
        parts.append((ring(gate_send, 1), ring(long_send, -1), feats))
    kept = None
    for chunk, part in zip(CHUNKS, parts):
        kept = main_call(
            chunk, *part, upstream, source, tail, params, masks, unshifts,
            sends, per_shard, kept,
        )
    mixed, grad_source, short_sums, lag_sums, skip_sums, head, end = kept
    head = ring(head[:, : SHORT - 1], -1)

    skip_slabs = C // LANES // shards
    skip_sums = skip_sums.reshape(shards, skip_slabs, 1, LANES)
    short_sums = short_sums.reshape(shards, -1, 8, LANES)
    room = ((0, 0), (0, short_sums.shape[1] - skip_slabs), (7, 0), (0, 0))
    short_sums = short_sums + jnp.pad(skip_sums, room)
    sums = jnp.concatenate(
        [short_sums.reshape(shards, -1, LANES), lag_sums.reshape(shards, -1, LANES)], axis=1
    )
    piece = sums.shape[1] // count
    sums = sums.reshape(shards * count, piece, LANES)
    sums = lax.all_to_all(sums.astype(bf16), ("fsdp", "ctx"), 0, 0, tiled=True)
    sums = jnp.sum(sums.astype(f32), axis=0)
    sums = sums * (float(shards * count * TOK) ** -0.5)
    grad_source = patch_call(starts[0], grad_source, end, head, params)
    sums = lax.all_to_all(
        jnp.broadcast_to(sums[None], (count,) + sums.shape), "ctx", 0, 0, tiled=True
    ).reshape(count * piece, LANES)
    slabs = 3 * C // LANES // shards
    grad_short = sums[: slabs * 8].reshape(slabs, 8, LANES)
    grad_skip = grad_short[:skip_slabs, 7].reshape(-1)
    grad_short = grad_short[:, :SHORT].transpose(1, 0, 2).reshape(SHORT, -1)
    grad_long = sums[slabs * 8 :].T
    return mixed[None], grad_source[None], grad_short, grad_long, grad_skip


def solution(mesh):
    placed = (
        P("fsdp", "ctx", None),
        P(None, "fsdp"),
        P(None, "fsdp"),
        P("fsdp"),
        P("fsdp", "ctx", None),
        P("fsdp", "ctx", None),
    )
    return jax.shard_map(
        body,
        mesh=mesh,
        in_specs=placed,
        out_specs=(
            P("fsdp", "ctx", None),
            P("fsdp", "ctx", None),
            P(None, "fsdp"),
            P(None, "fsdp"),
            P("fsdp"),
        ),
        check_vma=False,
    )
```
